128 devices in a mesh: row: 8 (over x_lo, y), col: 16 (over z, x_hi, core).
Axes of the slice: x: 4 (x_hi: 2, x_lo: 2; x = x_hi * 2 + x_lo), y: 4, z: 4, core: 2. Of those that a mesh axis runs over, the one named last changes fastest.
Arguments:
- hidden: bfloat16 [2048, 36864], P('col', 'row'), may hold values from -6 to 6
- weight: bfloat16 [36864, 4608], P('row', 'col'), may hold values from -0.03125 to 0.03125
- scale_exp: int32 [384, 48], P('row', 'col'), may hold values from -14 to -8
- teacher: bfloat16 [2048, 4608], P(('row', 'col')), may hold values from -6 to 6
Outputs:
- student_out: bfloat16 [2048, 4608], P('row', 'col')
- weight_grad: bfloat16 [36864, 4608], P('row', 'col')
The draws below stay inside these ranges and needn't reach their ends.
Inputs may be any that keep to these rules, and one draw needn't show every extreme that they name: `scale_exp`: integer exponents.
All inputs are finite; a program needn't handle non-finite values.
Results may differ from the reference program's by a relative error of at most 0.0065.
Values may be sent and summed in bfloat16 or wider, within the bound.
A program may use at most 128 MiB of HBM per device.

```python
import math
import jax
import jax.numpy as jnp

D = 4608
FF = 36864
TILE = 96
TOKENS = 2048


def touch_ends(result, own_key, least, top_value):
    longest = result.shape.index(max(result.shape))
    spots = []
    for shift in (0, 1):
        where = [jax.random.randint(jax.random.fold_in(own_key, axis), (), 0, length) for axis, length in enumerate(result.shape)]
        where[longest] = (where[longest] + shift) % result.shape[longest]
        spots.append(tuple(where))
    return result.at[spots[0]].set(least).at[spots[1]].set(top_value)


def block_scale(own_key, dims, pieces, low, top_value):
    gain = 1.0
    for dim, parts in pieces:
        draws = jax.random.uniform(jax.random.fold_in(jax.random.fold_in(own_key, 6), dim), (parts,), jnp.float32, low / len(pieces), top_value / len(pieces))
        gain = gain * jnp.repeat(jnp.exp(draws), dims[dim] // parts).reshape((-1,) + (1,) * (len(dims) - 1 - dim))
    return gain


def gaussian(own_key, dims, deviation, bound, shards=(), held_as=jnp.bfloat16):
    result = deviation * jax.random.normal(own_key, dims, jnp.float32)
    if shards:
        result = result * block_scale(own_key, dims, shards, -0.22, 0.18)
    return jnp.clip(result, -bound, bound).astype(held_as)


def setup_inputs(seed: int = 0) -> dict:
    arg_keys = jax.random.split(jax.random.key(seed), 5)
    hidden = gaussian(arg_keys[0], (TOKENS, FF), 1.0, 6.0, ((0, 16), (1, 8)))
    weight = gaussian(arg_keys[1], (FF, D), FF ** -0.5, 0.03125, ((0, 8), (1, 16)))
    scale_exp = touch_ends(jax.random.randint(arg_keys[2], (FF // TILE, D // TILE), -14, -7), jax.random.fold_in(arg_keys[2], 1), -14, (-7) - 1).astype(jnp.int32)
    teacher = gaussian(arg_keys[3], (TOKENS, D), 1.0, 6.0, ((0, 128),))
    return dict(hidden=hidden, weight=weight, scale_exp=scale_exp, teacher=teacher)


def quantize(weight, scale_exp):
    tile_rows = weight.shape[0] // scale_exp.shape[0]
    step_size = jnp.left_shift(jnp.int32(1), (scale_exp + 14).astype(jnp.int32)).astype(jnp.float32) * 2.0 ** (-14)
    inverse = jnp.left_shift(jnp.int32(1), (-8 - scale_exp).astype(jnp.int32)).astype(jnp.float32) * 256.0
    step_cols = jnp.repeat(step_size, tile_rows, axis=1)
    inverse_cols = jnp.repeat(inverse, tile_rows, axis=1)
    grouped = weight.astype(jnp.float32).reshape(scale_exp.shape[0], tile_rows, weight.shape[1])
    levels = jnp.floor(grouped * inverse_cols[:, None, :] + 0.5)
    keep_mask = (jnp.abs(levels) <= 127.0).astype(jnp.float32).reshape(weight.shape)
    quantized = (jnp.clip(levels, -127.0, 127.0) * step_cols[:, None, :]).reshape(weight.shape).astype(jnp.bfloat16)
    return (quantized, keep_mask)

def reference(hidden, weight, scale_exp, teacher):
    quantized, keep_mask = quantize(weight, scale_exp)
    student = jnp.dot(hidden, quantized, preferred_element_type=jnp.float32)
    factor = 1.0 / math.sqrt(TOKENS)
    grad_out = ((student - teacher.astype(jnp.float32)) * factor).astype(jnp.bfloat16)
    product = jnp.dot(hidden.T, grad_out, preferred_element_type=jnp.float32)
    return (student.astype(jnp.bfloat16), (product * keep_mask).astype(jnp.bfloat16))
```

```python
import functools
import math

import jax
import jax.numpy as jnp
from jax import lax
from jax.experimental import pallas as pl
from jax.experimental.pallas import tpu as pltpu
from jax.sharding import PartitionSpec as P

MESH = pl.DeviceIdType.MESH
BF16, F32 = jnp.bfloat16, jnp.float32
TILE = 96
CHUNK = 32
PIECE = 16

OWN, DOWN, UP, FAR = (0, 0), (-1, 0), (1, 0), (2, 0)
SIDE, SIDE_DOWN, SIDE_UP, SIDE_FAR = (0, 1), (-1, 1), (1, 1), (2, 1)
GROUPS = (
    ((*OWN, 0), (*OWN, 1)),
    ((*OWN, 2), (*OWN, 3)),
    ((*DOWN, 0), (*UP, 0)),
    ((*DOWN, 1), (*UP, 1)),
    ((*SIDE, 0), (*SIDE, 1)),
    ((*DOWN, 2), (*UP, 2)),
    ((*DOWN, 3), (*UP, 3)),
    ((*SIDE, 2), (*SIDE, 3)),
    ((*FAR, 0), (*FAR, 2)),
    ((*FAR, 1), (*FAR, 3)),
    ((*SIDE_DOWN, 0), (*SIDE_UP, 0)),
    ((*SIDE_DOWN, 1), (*SIDE_UP, 1)),
    ((*SIDE_FAR, 0), (*SIDE_FAR, 2)),
    ((*SIDE_DOWN, 2), (*SIDE_UP, 2)),
    ((*SIDE_FAR, 1), (*SIDE_FAR, 3)),
    ((*SIDE_DOWN, 3), (*SIDE_UP, 3)),
)
PLACE = {chunk: 4 * g + 2 * j for g, pair in enumerate(GROUPS) for j, chunk in enumerate(pair)}
STEPS = ((0, 2), (2, 3), (5, 3), (8, 2), (10, 3), (13, 2), (15, 1))
SEND_UP = (
    [((*OWN, c), (*DOWN, c)) for c in range(4)]
    + [((*DOWN, c), (*FAR, c)) for c in (0, 1)]
    + [((*SIDE, c), (*SIDE_DOWN, c)) for c in range(4)]
)
SEND_DOWN = (
    [((*OWN, c), (*UP, c)) for c in range(4)]
    + [((*UP, c), (*FAR, c)) for c in (2, 3)]
    + [((*SIDE, c), (*SIDE_UP, c)) for c in range(4)]
)
SEND_SIDE = [((*OWN, c), (*SIDE, c)) for c in range(4)] + [
    ((*FAR, c), (*SIDE_FAR, c)) for c in (0, 2, 1, 3)
]
START_UP = (0, 0, 1, 2, 3, 4, 5, 6, 7, 8)
START_DOWN = (0, 0, 1, 2, 3, 4, 5, 6, 7, 8)
START_SIDE = (0, 0, 1, 2, 5, 5, 6, 6)
ARRIVE_SIDE = (1, 2, 3, 4, 7, 8, 9, 9)
ARRIVALS = (
    [(*OWN, c) for c in range(4)]
    + [there for _, there in SEND_UP]
    + [there for _, there in SEND_DOWN]
    + [there for _, there in SEND_SIDE]
)
NUMBER = {chunk: i for i, chunk in enumerate(ARRIVALS)}
PLAN = (
    ("q", "a0"),
    ("b0",),
    ("a1", "c0"),
    ("d0", "b1"),
    ("a2", "e0", "c1"),
    ("b2", "d1"),
    ("a3", "e1", "c2"),
    ("b3", "d2"),
    ("a4", "e2", "c3"),
    ("a5", "b4", "d3", "e3", "c4", "b5"),
    ("a6", "d4", "c5", "b6", "e4", "c6", "d5", "d6", "e5", "e6"),
)


def kernel(
    factor,
    hidden, weight, scale, teacher,
    student_out, grad,
    held, keep, quant, total, parts, got_y, swap, got_x, grads, pieces, placed, cols, targets,
    up_s, up_r, down_s, down_r, side_s, side_r, core_s, core_r, load_s,
    part_s, part_r, swap_s, swap_r, gy_s, gy_r, gx_s, gx_r, fy_s, fy_r, out_s, out_r,
    col_s, col_r, row_s, row_r,
):
    row, col = lax.axis_index("row"), lax.axis_index("col")
    x_lo, y = row // 4, row % 4
    z, x_hi, core = col // 4, (col // 2) % 2, col % 2
    width = parts.shape[-1]
    depth = held.shape[-1]

    def in_col(dz, p, dc):
        return (row, ((z + dz + 4) % 4) * 4 + ((x_hi + p) % 2) * 2 + (core + dc) % 2)

    def in_row(dx, dy):
        return (((x_lo + dx) % 2) * 4 + (y + dy) % 4, col)

    def remote(src, dst, send, recv, device):
        return pltpu.make_async_remote_copy(
            src_ref=src, dst_ref=dst, send_sem=send, recv_sem=recv, device_id=device, device_id_type=MESH
        )

    up, down, side, sibling = in_col(1, 0, 0), in_col(-1, 0, 0), in_col(0, 1, 0), in_col(0, 0, 1)
    partner = in_row(1, 0)

    barrier = pltpu.get_barrier_semaphore()
    for k in range(1, 16):
        pl.semaphore_signal(barrier, inc=1, device_id=(row, (col + k) % 16), device_id_type=MESH)
    for k in range(1, 8):
        pl.semaphore_signal(barrier, inc=1, device_id=in_row(k // 4, k % 4), device_id_type=MESH)

    own = []
    for c in range(4):
        own.append(
            pltpu.make_async_copy(
                hidden.at[c], held.at[PLACE[(*OWN, c)] + core], load_s.at[c]
            )
        )
        own[c].start()
    load_weight = pltpu.make_async_copy(weight, keep, load_s.at[4])
    load_weight.start()
    pl.semaphore_wait(barrier, 22)

    sends = []

    def chunk_at(chunk):
        if chunk[:2] == OWN:
            return hidden.at[chunk[2]]
        return held.at[PLACE[chunk] + core]

    def stream(plan, send, recv, device):
        return [
            remote(chunk_at(here), held.at[PLACE[there] + core], send.at[i], recv.at[i], device)
            for i, (here, there) in enumerate(plan)
        ]

    ups = stream(SEND_UP, up_s, up_r, up)
    downs = stream(SEND_DOWN, down_s, down_r, down)
    sides = stream(SEND_SIDE, side_s, side_r, side)
    across = [
        remote(
            chunk_at(chunk), held.at[PLACE[chunk] + core], core_s.at[i], core_r.at[i], sibling
        )
        for i, chunk in enumerate(ARRIVALS)
    ]

    def start(copy):
        copy.start()
        sends.append(copy)

    def start_tick(tick):
        for copies, ticks in ((ups, START_UP), (downs, START_DOWN), (sides, START_SIDE)):
            for copy, at in zip(copies, ticks):
                if at == tick:
                    start(copy)

    t_core, t_chunk, t_half = col // 8, (col % 8) // 2, col % 2
    t_place = (2 * t_core + t_half) * 4 + t_chunk
    t_cols = [
        remote(
            teacher.at[(col + k) % 16],
            cols.at[t_place],
            col_s.at[k - 1],
            col_r.at[k - 1],
            (row, (col + k) % 16),
        )
        for k in range(1, 16)
    ]
    t_own = pltpu.make_async_copy(teacher.at[col], cols.at[t_place], load_s.at[5])
    t_rows = [
        remote(
            cols.at[pl.ds(((y + k % 4) % 4) * 4, 4)],
            targets.at[row],
            row_s.at[k - 1],
            row_r.at[k - 1],
            in_row(k // 4, k % 4),
        )
        for k in range(1, 8)
    ]

    def quantize():
        load_weight.wait()
        lane = lax.broadcasted_iota(jnp.int32, (8, width), 1)

        @pl.loop(0, depth // TILE)
        def _(i):
            e = jnp.where(lane < TILE, scale[i, 0], jnp.where(lane < 2 * TILE, scale[i, 1], scale[i, 2]))
            step = (jnp.left_shift(jnp.int32(1), e + 14).astype(F32) * 2.0 ** (-14))[0:1]
            inverse = (jnp.left_shift(jnp.int32(1), -8 - e).astype(F32) * 256.0)[0:1]
            rows = pl.ds(pl.multiple_of(i * TILE, TILE), TILE)
            levels = jnp.floor(keep[rows].astype(F32) * inverse + 0.5)
            quant[rows] = (jnp.clip(levels, -127.0, 127.0) * step).astype(BF16)
            keep[rows] = (jnp.abs(levels) <= 127.0).astype(F32).astype(BF16)

    def chunks_of(step):
        first, count = STEPS[step]
        return [chunk for g in range(first, first + count) for chunk in GROUPS[g]]

    def part_copies(s):
        first, count = STEPS[s]
        return [
            remote(
                parts.at[(y + k) % 4, :, pl.ds(first, count)],
                got_y.at[k - 1, :, pl.ds(first, count)],
                part_s.at[s, k - 1],
                part_r.at[s, k - 1],
                in_row(0, k),
            )
            for k in range(1, 4)
        ]

    def swap_copy(s):
        groups = pl.ds(*STEPS[s])
        return remote(swap.at[groups], got_x.at[groups], swap_s.at[s], swap_r.at[s], partner)

    def grad_copies(s):
        mine = grads.at[y, x_lo, pl.ds(*STEPS[s])]
        return [
            remote(mine, mine, gy_s.at[s, k - 1], gy_r.at[s, k - 1], in_row(0, k))
            for k in range(1, 4)
        ] + [remote(mine, mine, gx_s.at[s], gx_r.at[s], partner)]

    def forward_copies(s):
        theirs = grads.at[y, 1 - x_lo, pl.ds(*STEPS[s])]
        return [
            remote(theirs, theirs, fy_s.at[s, k - 1], fy_r.at[s, k - 1], in_row(0, k))
            for k in range(1, 4)
        ]

    def stage_a(s):
        for chunk in chunks_of(s):
            across[NUMBER[chunk]].wait_recv()
        first, count = STEPS[s]

        @pl.loop(first, first + count)
        def _(g):
            tokens = held[pl.ds(g * 4, 4)].reshape(4 * CHUNK, depth)
            part = jnp.dot(tokens, quant[...], preferred_element_type=F32).astype(BF16)
            for m in range(8):
                parts[m % 4, m // 4, g] = part[m * PIECE : (m + 1) * PIECE]

        for copy in part_copies(s):
            start(copy)

    def over_y(x, g):
        value = parts[y, x, g].astype(F32)
        for k in range(3):
            value = value + got_y[k, x, g].astype(F32)
        return value

    def stage_b(s):
        for copy in part_copies(s):
            copy.wait_recv()
        first, count = STEPS[s]
        for g in range(first, first + count):
            swap[g] = over_y(1 - x_lo, g).astype(BF16)
        start(swap_copy(s))

    def where_from(g):
        (dz0, p0, c0), (dz1, p1, c1) = GROUPS[g]
        t0 = ((z + dz0 + 4) % 4) * 2 + (x_hi + p0) % 2
        t1 = ((z + dz1 + 4) % 4) * 2 + (x_hi + p1) % 2
        return t0 + x_lo * (t1 - t0), c0 + x_lo * (c1 - c0)

    def piece_copy(g):
        t, c = where_from(g)
        spot = (y // 2) * 8 + 2 * c + y % 2
        return t, (
            pltpu.make_async_copy(pieces.at[g], placed.at[spot], out_r.at[spot]),
            remote(pieces.at[g], placed.at[spot], out_s.at[g], out_r.at[spot], (t, col)),
        )

    def stage_c(s):
        swap_copy(s).wait_recv()
        first, count = STEPS[s]
        for g in range(first, first + count):
            t, c = where_from(g)
            student = over_y(x_lo, g) + got_x[g].astype(F32)
            pieces[g] = student.astype(BF16)
            grads[y, x_lo, g] = ((student - targets[t, c].astype(F32)) * factor).astype(BF16)
        for copy in grad_copies(s):
            start(copy)
        for g in range(first, first + count):
            t, (here, there) = piece_copy(g)

            @pl.when(t == row)
            def _():
                here.start()

            @pl.when(t != row)
            def _():
                there.start()

    def stage_d(s):
        grad_copies(s)[3].wait_recv()
        for copy in forward_copies(s):
            start(copy)

    def stage_e(s):
        for copy in grad_copies(s)[:3] + forward_copies(s):
            copy.wait_recv()
        first, count = STEPS[s]
        g_t = jnp.concatenate(
            [grads[m % 4, m // 4, g] for g in range(first, first + count) for m in range(8)], axis=0
        ).T

        @pl.loop(0, depth // 512)
        def _(i):
            ff = pl.ds(pl.multiple_of(i * 512, 512), 512)
            tokens = held[pl.ds(4 * first, 4 * count), :, ff].reshape(4 * CHUNK * count, 512)
            part = jnp.dot(g_t, tokens, preferred_element_type=F32)
            if s == 0:
                total[:, ff] = part
            else:
                total[:, ff] += part

    stages = {"a": stage_a, "b": stage_b, "c": stage_c, "d": stage_d, "e": stage_e}

    start_tick(0)
    for copy in t_cols:
        start(copy)
    t_own.start()
    for c in range(4):
        start(across[c])

    for tick in range(11):
        if tick:
            arrived = [ups[tick - 1], downs[tick - 1]]
            names = [SEND_UP[tick - 1][1], SEND_DOWN[tick - 1][1]]
            for i, at in enumerate(ARRIVE_SIDE):
                if at == tick:
                    arrived.append(sides[i])
                    names.append(SEND_SIDE[i][1])
            for copy in arrived:
                copy.wait_recv()
            start_tick(tick)
            for name in names:
                start(across[NUMBER[name]])
        if tick == 1:
            t_own.wait()
            for copy in t_cols:
                copy.wait_recv()
            for copy in t_rows:
                start(copy)
            targets[row] = cols[pl.ds(y * 4, 4)]
        if tick == 2:
            for copy in t_rows:
                copy.wait_recv()
        for what in PLAN[tick]:
            if what == "q":
                quantize()
                for copy in own:
                    copy.wait()
            else:
                stages[what[0]](int(what[1]))

    out = quant
    writes = []
    span = 512
    for i in range(depth // span):
        ff = slice(i * span, (i + 1) * span)
        out[ff] = (total[:, ff].T * keep[ff].astype(F32)).astype(BF16)
        writes.append(pltpu.make_async_copy(out.at[pl.ds(i * span, span)], grad.at[pl.ds(i * span, span)], load_s.at[6 + i]))
        writes[-1].start()
    for spot in range(16):
        pltpu.make_async_copy(pieces.at[0], placed.at[spot], out_r.at[spot]).wait()
    write = pltpu.make_async_copy(placed, student_out, load_s.at[5])
    write.start()
    for g in range(16):
        t, (here, there) = piece_copy(g)

        @pl.when(t != row)
        def _():
            there.wait_send()

    for copy in sends:
        copy.wait_send()
    write.wait()
    for copy in writes:
        copy.wait()


def local(hidden, weight, scale_exp, teacher):
    block, depth = hidden.shape
    width = weight.shape[1]
    tokens = block * lax.axis_size("col")
    groups, steps = len(GROUPS), len(STEPS)
    hidden = hidden.reshape(block // CHUNK, CHUNK, depth)
    teacher = teacher.reshape(PIECE, -1, width).transpose(1, 0, 2)
    dma = pltpu.SemaphoreType.DMA
    anywhere = pl.BlockSpec(memory_space=pl.ANY)
    student_out, grad = pl.pallas_call(
        functools.partial(kernel, 1.0 / math.sqrt(tokens)),
        out_shape=(
            jax.ShapeDtypeStruct((16, PIECE, width), BF16),
            jax.ShapeDtypeStruct((depth, width), BF16),
        ),
        in_specs=[anywhere, anywhere, pl.BlockSpec(memory_space=pltpu.SMEM), anywhere],
        out_specs=(anywhere, anywhere),
        scratch_shapes=[
            pltpu.VMEM((4 * groups, CHUNK, depth), BF16),
            pltpu.VMEM((depth, width), BF16),
            pltpu.VMEM((depth, width), BF16),
            pltpu.VMEM((width, depth), F32),
            pltpu.VMEM((4, 2, groups, PIECE, width), BF16),
            pltpu.VMEM((3, 2, groups, PIECE, width), BF16),
            pltpu.VMEM((groups, PIECE, width), BF16),
            pltpu.VMEM((groups, PIECE, width), BF16),
            pltpu.VMEM((4, 2, groups, PIECE, width), BF16),
            pltpu.VMEM((groups, PIECE, width), BF16),
            pltpu.VMEM((16, PIECE, width), BF16),
            pltpu.VMEM((16, PIECE, width), BF16),
            pltpu.VMEM((8, 4, PIECE, width), BF16),
            dma((10,)), dma((10,)), dma((10,)), dma((10,)), dma((8,)), dma((8,)),
            dma((32,)), dma((32,)), dma((16,)),
            dma((steps, 3)), dma((steps, 3)), dma((steps,)), dma((steps,)),
            dma((steps, 3)), dma((steps, 3)), dma((steps,)), dma((steps,)),
            dma((steps, 3)), dma((steps, 3)), dma((groups,)), dma((16,)),
            dma((15,)), dma((15,)), dma((7,)), dma((7,)),
        ],
        compiler_params=pltpu.CompilerParams(
            collective_id=0, has_side_effects=True, vmem_limit_bytes=56 * 2**20
        ),
        cost_estimate=pl.CostEstimate(
            flops=4 * tokens * depth * width, bytes_accessed=3 * depth * width, transcendentals=0
        ),
    )(hidden, weight, scale_exp, teacher)
    return (student_out.reshape(16 * PIECE, width), grad)


def solution(mesh):
    placed = (P("col", "row"), P("row", "col"), P("row", "col"), P(("row", "col"), None))
    return jax.shard_map(
        local,
        mesh=mesh,
        in_specs=placed,
        out_specs=(P("row", "col"), P("row", "col")),
        check_vma=False,
    )
```

```python
import functools
import math

import jax
import jax.numpy as jnp
from jax import lax
from jax.experimental import pallas as pl
from jax.experimental.pallas import tpu as pltpu
from jax.sharding import PartitionSpec as P

MESH = pl.DeviceIdType.MESH
BF16, F32 = jnp.bfloat16, jnp.float32
TILE = 96
CHUNK = 32
PIECE = 16

OWN, DOWN, UP, FAR = (0, 0), (-1, 0), (1, 0), (2, 0)
SIDE, SIDE_DOWN, SIDE_UP, SIDE_FAR = (0, 1), (-1, 1), (1, 1), (2, 1)
GROUPS = (
    ((*OWN, 0), (*OWN, 1)),
    ((*OWN, 2), (*OWN, 3)),
    ((*DOWN, 0), (*UP, 0)),
    ((*DOWN, 1), (*UP, 1)),
    ((*SIDE, 0), (*SIDE, 1)),
    ((*SIDE, 2), (*SIDE, 3)),
    ((*DOWN, 2), (*UP, 2)),
    ((*DOWN, 3), (*UP, 3)),
    ((*FAR, 0), (*FAR, 2)),
    ((*FAR, 1), (*FAR, 3)),
    ((*SIDE_DOWN, 0), (*SIDE_UP, 0)),
    ((*SIDE_DOWN, 1), (*SIDE_UP, 1)),
    ((*SIDE_FAR, 0), (*SIDE_FAR, 2)),
    ((*SIDE_FAR, 1), (*SIDE_FAR, 3)),
    ((*SIDE_DOWN, 2), (*SIDE_UP, 2)),
    ((*SIDE_DOWN, 3), (*SIDE_UP, 3)),
)
PLACE = {chunk: 4 * g + 2 * j for g, pair in enumerate(GROUPS) for j, chunk in enumerate(pair)}
STEPS = ((0, 2), (2, 2), (4, 2), (6, 2), (8, 2), (10, 2), (12, 2), (14, 1), (15, 1))
SEND_UP = (
    [((*OWN, c), (*DOWN, c)) for c in range(4)]
    + [((*DOWN, c), (*FAR, c)) for c in (0, 1)]
    + [((*SIDE, c), (*SIDE_DOWN, c)) for c in range(4)]
)
SEND_DOWN = (
    [((*OWN, c), (*UP, c)) for c in range(4)]
    + [((*UP, c), (*FAR, c)) for c in (2, 3)]
    + [((*SIDE, c), (*SIDE_UP, c)) for c in range(4)]
)
SEND_SIDE = [((*OWN, c), (*SIDE, c)) for c in range(4)] + [
    ((*FAR, c), (*SIDE_FAR, c)) for c in (0, 2, 1, 3)
]
START_UP = (0, 0, 1, 2, 3, 4, 5, 6, 7, 8)
START_DOWN = (0, 0, 1, 2, 3, 4, 5, 6, 7, 8)
START_SIDE = (0, 0, 1, 2, 5, 5, 6, 6)
ARRIVE_SIDE = (1, 2, 3, 4, 7, 8, 9, 9)
ARRIVALS = (
    [(*OWN, c) for c in range(4)]
    + [there for _, there in SEND_UP]
    + [there for _, there in SEND_DOWN]
    + [there for _, there in SEND_SIDE]
)
NUMBER = {chunk: i for i, chunk in enumerate(ARRIVALS)}
PLAN = (
    "t q a0",
    "b0",
    "a1",
    "c0 b1",
    "a2 a3",
    "d0 c1 b2 b3",
    "a4 e0",
    "d1 c2 c3 b4",
    "a5 e1",
    "a6 a7 d2 d3 c4 b5",
    "a8 b6 b7 c5 d4 e2 b8 c6 c7 d5 e3 c8 d6 d7 e4 e5 d8 e6 f",
)


def kernel(
    factor,
    hidden, weight, scale, teacher,
    student_out, grad,
    held, keep, quant, total, whole, spread, parts, got_y, swap, got_x, grads, pieces, placed, turned, cols, targets,
    up_s, up_r, down_s, down_r, side_s, side_r, core_s, core_r, load_s,
    part_s, part_r, swap_s, swap_r, gy_s, gy_r, gx_s, gx_r, fy_s, fy_r, out_s, out_r,
    col_s, col_r, row_s, row_r,
):
    row, col = lax.axis_index("row"), lax.axis_index("col")
    x_lo, y = row // 4, row % 4
    z, x_hi, core = col // 4, (col // 2) % 2, col % 2
    width = parts.shape[-1]
    depth = held.shape[-1]
    steps = len(STEPS)

    def in_col(dz, p, dc):
        return (row, ((z + dz + 4) % 4) * 4 + ((x_hi + p) % 2) * 2 + (core + dc) % 2)

    def in_row(dx, dy):
        return (((x_lo + dx) % 2) * 4 + (y + dy) % 4, col)

    def remote(src, dst, send, recv, device):
        return pltpu.make_async_remote_copy(
            src_ref=src, dst_ref=dst, send_sem=send, recv_sem=recv, device_id=device, device_id_type=MESH
        )

    up, down, side, sibling = in_col(1, 0, 0), in_col(-1, 0, 0), in_col(0, 1, 0), in_col(0, 0, 1)
    partner = in_row(1, 0)

    barrier = pltpu.get_barrier_semaphore()
    for k in range(1, 16):
        pl.semaphore_signal(barrier, inc=1, device_id=(row, (col + k) % 16), device_id_type=MESH)
    for k in range(1, 8):
        pl.semaphore_signal(barrier, inc=1, device_id=in_row(k // 4, k % 4), device_id_type=MESH)

    own = []
    for c in range(4):
        own.append(
            pltpu.make_async_copy(
                hidden.at[c], held.at[PLACE[(*OWN, c)] + core], load_s.at[c]
            )
        )
        own[c].start()
    load_weight = pltpu.make_async_copy(weight, keep, load_s.at[4])
    load_weight.start()
    load_teacher = pltpu.make_async_copy(teacher, whole, load_s.at[6])
    load_teacher.start()
    pl.semaphore_wait(barrier, 22)

    sends = []

    def chunk_at(chunk):
        if chunk[:2] == OWN:
            return hidden.at[chunk[2]]
        return held.at[PLACE[chunk] + core]

    def stream(plan, send, recv, device):
        return [
            remote(chunk_at(here), held.at[PLACE[there] + core], send.at[i], recv.at[i], device)
            for i, (here, there) in enumerate(plan)
        ]

    ups = stream(SEND_UP, up_s, up_r, up)
    downs = stream(SEND_DOWN, down_s, down_r, down)
    sides = stream(SEND_SIDE, side_s, side_r, side)
    across = [
        remote(
            chunk_at(chunk), held.at[PLACE[chunk] + core], core_s.at[i], core_r.at[i], sibling
        )
        for i, chunk in enumerate(ARRIVALS)
    ]

    def start(copy):
        copy.start()
        sends.append(copy)

    def start_tick(tick):
        for copies, ticks in ((ups, START_UP), (downs, START_DOWN), (sides, START_SIDE)):
            for copy, at in zip(copies, ticks):
                if at == tick:
                    start(copy)

    t_core, t_chunk, t_half = col // 8, (col % 8) // 2, col % 2
    t_place = (2 * t_core + t_half) * 4 + t_chunk
    t_cols = [
        remote(
            spread.at[(col + k) % 16],
            cols.at[t_place],
            col_s.at[k - 1],
            col_r.at[k - 1],
            (row, (col + k) % 16),
        )
        for k in range(1, 16)
    ]
    t_own = pltpu.make_async_copy(spread.at[col], cols.at[t_place], load_s.at[5])
    t_rows = [
        remote(
            cols.at[pl.ds(((y + k % 4) % 4) * 4, 4)],
            targets.at[row],
            row_s.at[k - 1],
            row_r.at[k - 1],
            in_row(k // 4, k % 4),
        )
        for k in range(1, 8)
    ]

    def spread_teacher():
        load_teacher.wait()
        for i in range(16):
            spread[i] = whole[:, i * width : (i + 1) * width]
        for copy in t_cols:
            start(copy)
        t_own.start()

    def quantize():
        load_weight.wait()
        span = 4 * TILE
        lane = lax.broadcasted_iota(jnp.int32, (8, span), 1)

        @pl.loop(0, depth // span)
        def _(i):
            ff = pl.ds(pl.multiple_of(i * span, span), span)
            for j in range(width // TILE):
                e = jnp.full((8, span), scale[j, 4 * i], jnp.int32)
                for k in range(1, 4):
                    e = jnp.where(lane < k * TILE, e, scale[j, 4 * i + k])
                step = (jnp.left_shift(jnp.int32(1), e + 14).astype(F32) * 2.0 ** (-14))[0:1]
                inverse = (jnp.left_shift(jnp.int32(1), -8 - e).astype(F32) * 256.0)[0:1]
                rows = slice(j * TILE, (j + 1) * TILE)
                levels = jnp.floor(keep[rows, ff].astype(F32) * inverse + 0.5)
                quant[rows, ff] = (jnp.clip(levels, -127.0, 127.0) * step).astype(BF16)
                keep[rows, ff] = (jnp.abs(levels) <= 127.0).astype(F32).astype(BF16)

    def chunks_of(step):
        first, count = STEPS[step]
        return [chunk for g in range(first, first + count) for chunk in GROUPS[g]]

    def part_copies(s):
        first, count = STEPS[s]
        return [
            remote(
                parts.at[(y + k) % 4, :, pl.ds(first, count)],
                got_y.at[k - 1, :, pl.ds(first, count)],
                part_s.at[s, k - 1],
                part_r.at[s, k - 1],
                in_row(0, k),
            )
            for k in range(1, 4)
        ]

    def swap_copy(s):
        groups = pl.ds(*STEPS[s])
        return remote(swap.at[groups], got_x.at[groups], swap_s.at[s], swap_r.at[s], partner)

    def grad_copies(s):
        mine = grads.at[y, x_lo, pl.ds(*STEPS[s])]
        return [
            remote(mine, mine, gy_s.at[s, k - 1], gy_r.at[s, k - 1], in_row(0, k))
            for k in range(1, 4)
        ] + [remote(mine, mine, gx_s.at[s], gx_r.at[s], partner)]

    def forward_copies(s):
        theirs = grads.at[y, 1 - x_lo, pl.ds(*STEPS[s])]
        return [
            remote(theirs, theirs, fy_s.at[s, k - 1], fy_r.at[s, k - 1], in_row(0, k))
            for k in range(1, 4)
        ]

    def tokens_of(first, count, ff):
        return held[4 * first : 4 * (first + count), :, ff].reshape(4 * CHUNK * count, -1)

    def stage_a(s):
        for chunk in chunks_of(s):
            across[NUMBER[chunk]].wait_recv()
        first, count = STEPS[s]

        part = lax.dot_general(
            quant[...], tokens_of(first, count, slice(None)), (((1,), (1,)), ((), ())),
            preferred_element_type=F32,
        ).T.astype(BF16)
        for g in range(count):
            for m in range(8):
                at = (g * 8 + m) * PIECE
                parts[m % 4, m // 4, first + g] = part[at : at + PIECE]

        for copy in part_copies(s):
            start(copy)

    def over_y(x, g):
        value = parts[y, x, g].astype(F32)
        for k in range(3):
            value = value + got_y[k, x, g].astype(F32)
        return value

    def stage_b(s):
        for copy in part_copies(s):
            copy.wait_recv()
        first, count = STEPS[s]
        for g in range(first, first + count):
            swap[g] = over_y(1 - x_lo, g).astype(BF16)
        start(swap_copy(s))

    def where_from(g):
        (dz0, p0, c0), (dz1, p1, c1) = GROUPS[g]
        t0 = ((z + dz0 + 4) % 4) * 2 + (x_hi + p0) % 2
        t1 = ((z + dz1 + 4) % 4) * 2 + (x_hi + p1) % 2
        return t0 + x_lo * (t1 - t0), c0 + x_lo * (c1 - c0)

    def piece_copy(g):
        t, c = where_from(g)
        spot = (y // 2) * 8 + 2 * c + y % 2
        return t, (
            pltpu.make_async_copy(pieces.at[g], placed.at[spot], out_r.at[spot]),
            remote(pieces.at[g], placed.at[spot], out_s.at[g], out_r.at[spot], (t, col)),
        )

    def stage_c(s):
        swap_copy(s).wait_recv()
        first, count = STEPS[s]
        for g in range(first, first + count):
            t, c = where_from(g)
            student = over_y(x_lo, g) + got_x[g].astype(F32)
            pieces[g] = student.astype(BF16)
            grads[y, x_lo, g] = ((student - targets[t, c].astype(F32)) * factor).astype(BF16)
        for copy in grad_copies(s):
            start(copy)
        for g in range(first, first + count):
            t, (here, there) = piece_copy(g)

            @pl.when(t == row)
            def _():
                here.start()

            @pl.when(t != row)
            def _():
                there.start()

    def stage_d(s):
        grad_copies(s)[3].wait_recv()
        for copy in forward_copies(s):
            start(copy)

    def gradients(first, count):
        pieces_of = [grads[m % 4, m // 4, g] for g in range(first, first + count) for m in range(8)]
        return jnp.concatenate(pieces_of, axis=0).T

    def wait_gradients(s):
        for copy in grad_copies(s)[:3] + forward_copies(s):
            copy.wait_recv()

    def stage_e(s):
        wait_gradients(s)
        first, count = STEPS[s]
        part = jnp.dot(gradients(first, count), tokens_of(first, count, slice(None)), preferred_element_type=F32)
        if s == 0:
            total[...] = part
        else:
            total[...] += part

    writes = []

    def finish():
        for s in (steps - 2, steps - 1):
            wait_gradients(s)
        first = STEPS[steps - 2][0]
        count = len(GROUPS) - first
        g_t = gradients(first, count)
        span = depth // 4
        for i in range(4):
            ff = slice(i * span, (i + 1) * span)
            part = jnp.dot(g_t, tokens_of(first, count, ff), preferred_element_type=F32)
            quant[:, ff] = ((total[:, ff] + part) * keep[:, ff].astype(F32)).astype(BF16)
            write = pltpu.make_async_copy(quant.at[:, ff], grad.at[:, ff], load_s.at[7 + i])
            write.start()
            writes.append(write)
        for spot in range(16):
            pltpu.make_async_copy(pieces.at[0], placed.at[spot], out_r.at[spot]).wait()
        turned[...] = placed[...].reshape(16 * PIECE, width).T
        write = pltpu.make_async_copy(turned, student_out, load_s.at[5])
        write.start()
        writes.append(write)

    stages = {"a": stage_a, "b": stage_b, "c": stage_c, "d": stage_d, "e": stage_e}

    start_tick(0)
    for c in range(4):
        start(across[c])

    for tick in range(11):
        if tick:
            arrived = [ups[tick - 1], downs[tick - 1]]
            names = [SEND_UP[tick - 1][1], SEND_DOWN[tick - 1][1]]
            for i, at in enumerate(ARRIVE_SIDE):
                if at == tick:
                    arrived.append(sides[i])
                    names.append(SEND_SIDE[i][1])
            for copy in arrived:
                copy.wait_recv()
            start_tick(tick)
            for name in names:
                start(across[NUMBER[name]])
        if tick == 1:
            t_own.wait()
            for copy in t_cols:
                copy.wait_recv()
            for copy in t_rows:
                start(copy)
            targets[row] = cols[pl.ds(y * 4, 4)]
        if tick == 2:
            for copy in t_rows:
                copy.wait_recv()
        for what in PLAN[tick].split():
            if what == "t":
                spread_teacher()
            elif what == "q":
                quantize()
                for copy in own:
                    copy.wait()
            elif what == "f":
                finish()
            else:
                stages[what[0]](int(what[1]))

    for g in range(16):
        t, (here, there) = piece_copy(g)

        @pl.when(t != row)
        def _():
            there.wait_send()

    for copy in sends:
        copy.wait_send()
    for copy in writes:
        copy.wait()


def local(hidden, weight, scale_exp, teacher):
    block, depth = hidden.shape
    width = weight.shape[1]
    tokens = block * lax.axis_size("col")
    groups, steps = len(GROUPS), len(STEPS)
    hidden = hidden.reshape(block // CHUNK, CHUNK, depth)
    dma = pltpu.SemaphoreType.DMA
    anywhere = pl.BlockSpec(memory_space=pl.ANY)
    student_out, grad = pl.pallas_call(
        functools.partial(kernel, 1.0 / math.sqrt(tokens)),
        out_shape=(
            jax.ShapeDtypeStruct((width, 16 * PIECE), BF16),
            jax.ShapeDtypeStruct((width, depth), BF16),
        ),
        in_specs=[anywhere, anywhere, pl.BlockSpec(memory_space=pltpu.SMEM), anywhere],
        out_specs=(anywhere, anywhere),
        scratch_shapes=[
            pltpu.VMEM((4 * groups, CHUNK, depth), BF16),
            pltpu.VMEM((width, depth), BF16),
            pltpu.VMEM((width, depth), BF16),
            pltpu.VMEM((width, depth), F32),
            pltpu.VMEM((16, depth), BF16),
            pltpu.VMEM((16, PIECE, width), BF16),
            pltpu.VMEM((4, 2, groups, PIECE, width), BF16),
            pltpu.VMEM((3, 2, groups, PIECE, width), BF16),
            pltpu.VMEM((groups, PIECE, width), BF16),
            pltpu.VMEM((groups, PIECE, width), BF16),
            pltpu.VMEM((4, 2, groups, PIECE, width), BF16),
            pltpu.VMEM((groups, PIECE, width), BF16),
            pltpu.VMEM((16, PIECE, width), BF16),
            pltpu.VMEM((width, 16 * PIECE), BF16),
            pltpu.VMEM((16, PIECE, width), BF16),
            pltpu.VMEM((8, 4, PIECE, width), BF16),
            dma((10,)), dma((10,)), dma((10,)), dma((10,)), dma((8,)), dma((8,)),
            dma((32,)), dma((32,)), dma((16,)),
            dma((steps, 3)), dma((steps, 3)), dma((steps,)), dma((steps,)),
            dma((steps, 3)), dma((steps, 3)), dma((steps,)), dma((steps,)),
            dma((steps, 3)), dma((steps, 3)), dma((groups,)), dma((16,)),
            dma((15,)), dma((15,)), dma((7,)), dma((7,)),
        ],
        compiler_params=pltpu.CompilerParams(
            collective_id=0, has_side_effects=True, vmem_limit_bytes=56 * 2**20
        ),
        cost_estimate=pl.CostEstimate(
            flops=4 * tokens * depth * width, bytes_accessed=3 * depth * width, transcendentals=0
        ),
    )(hidden, weight.T, scale_exp.T, teacher)
    return (student_out.T, grad.T)


def solution(mesh):
    placed = (P("col", "row"), P("row", "col"), P("row", "col"), P(("row", "col"), None))
    return jax.shard_map(
        local,
        mesh=mesh,
        in_specs=placed,
        out_specs=(P("row", "col"), P("row", "col")),
        check_vma=False,
    )
```

```python
import functools
import math

import jax
import jax.numpy as jnp
from jax import lax
from jax.experimental import pallas as pl
from jax.experimental.pallas import tpu as pltpu
from jax.sharding import PartitionSpec as P

MESH = pl.DeviceIdType.MESH
BF16, F32 = jnp.bfloat16, jnp.float32
TILE = 96
CHUNK = 32
PIECE = 16

OWN, DOWN, UP, FAR = (0, 0), (-1, 0), (1, 0), (2, 0)
SIDE, SIDE_DOWN, SIDE_UP, SIDE_FAR = (0, 1), (-1, 1), (1, 1), (2, 1)
GROUPS = (
    ((*OWN, 0), (*OWN, 1)),
    ((*OWN, 2), (*OWN, 3)),
    ((*DOWN, 0), (*UP, 2)),
    ((*DOWN, 1), (*UP, 3)),
    ((*SIDE, 0), (*SIDE, 1)),
    ((*SIDE, 2), (*SIDE, 3)),
    ((*FAR, 0), (*FAR, 2)),
    ((*FAR, 1), (*FAR, 3)),
    ((*DOWN, 2), (*UP, 0)),
    ((*DOWN, 3), (*UP, 1)),
    ((*SIDE_DOWN, 0), (*SIDE_UP, 0)),
    ((*SIDE_DOWN, 1), (*SIDE_UP, 1)),
    ((*SIDE_FAR, 0), (*SIDE_FAR, 2)),
    ((*SIDE_FAR, 1), (*SIDE_FAR, 3)),
    ((*SIDE_DOWN, 2), (*SIDE_UP, 2)),
    ((*SIDE_DOWN, 3), (*SIDE_UP, 3)),
)
PLACE = {chunk: 4 * g + 2 * j for g, pair in enumerate(GROUPS) for j, chunk in enumerate(pair)}
STEPS = ((0, 2), (2, 2), (4, 2), (6, 2), (8, 2), (10, 2), (12, 2), (14, 1), (15, 1))
SEND_UP = [
    ((*OWN, 0), (*DOWN, 0)),
    ((*OWN, 1), (*DOWN, 1)),
    ((*DOWN, 0), (*FAR, 0)),
    ((*OWN, 2), (*DOWN, 2)),
    ((*DOWN, 1), (*FAR, 1)),
    ((*OWN, 3), (*DOWN, 3)),
] + [((*SIDE, c), (*SIDE_DOWN, c)) for c in range(4)]
SEND_DOWN = [
    ((*OWN, 2), (*UP, 2)),
    ((*OWN, 3), (*UP, 3)),
    ((*UP, 2), (*FAR, 2)),
    ((*OWN, 0), (*UP, 0)),
    ((*UP, 3), (*FAR, 3)),
    ((*OWN, 1), (*UP, 1)),
] + [((*SIDE, c), (*SIDE_UP, c)) for c in range(4)]
SEND_SIDE = [((*OWN, c), (*SIDE, c)) for c in range(4)] + [
    ((*FAR, c), (*SIDE_FAR, c)) for c in (0, 2, 1, 3)
]
START_UP = (0, 0, 1, 2, 3, 4, 5, 6, 7, 8)
START_DOWN = (0, 0, 1, 2, 3, 4, 5, 6, 7, 8)
START_SIDE = (0, 1, 2, 3, 4, 5, 6, 7)
ARRIVE_SIDE = (2, 3, 4, 5, 6, 7, 8, 9)
ARRIVALS = (
    [(*OWN, c) for c in range(4)]
    + [there for _, there in SEND_UP]
    + [there for _, there in SEND_DOWN]
    + [there for _, there in SEND_SIDE]
)
NUMBER = {chunk: i for i, chunk in enumerate(ARRIVALS)}
PLAN = (
    ("q", "a0",),
    ("x",),
    ("rows", "b0", "x", "a1",),
    ("x",),
    ("targets", "c0", "b1", "x",),
    ("d0", "c1", "x", "a3", "a2",),
    ("d1", "x", "a4", "e0",),
    ("b3", "b2", "x", "e1",),
    ("c3", "c2", "b4", "a5",),
    ("d3", "d2", "c4", "a7", "a6",),
    ("d4", "b5", "a8", "b7", "b6", "e23", "c5", "c7", "c6", "r", "e4", "d5", "d7", "d6", "e56", "f",),
)


def kernel(
    factor,
    hidden, weight, scale, teacher,
    student_out, grad,
    held, keep, quant, total, whole, spread, parts, got_y, swap, got_x, got_last, grads, pieces, placed, cols, targets,
    load, sent, up_r, down_r, side_r, core_r, part_r, swap_r, grad_y_r, grad_x_r, out_s, out_r, last_r, teacher_r,
):
    row, col = lax.axis_index("row"), lax.axis_index("col")
    x_lo, y = row // 4, row % 4
    z, x_hi, core = col // 4, (col // 2) % 2, col % 2
    width = parts.shape[-1]
    depth = held.shape[-1]
    steps = len(STEPS)
    last = STEPS[-1][0]

    def in_col(dz, p, dc):
        return (row, ((z + dz + 4) % 4) * 4 + ((x_hi + p) % 2) * 2 + (core + dc) % 2)

    def in_row(dx, dy):
        return (((x_lo + dx) % 2) * 4 + (y + dy) % 4, col)

    def remote(src, dst, send, recv, device):
        return pltpu.make_async_remote_copy(
            src_ref=src, dst_ref=dst, send_sem=send, recv_sem=recv, device_id=device, device_id_type=MESH
        )

    up, down, side, sibling = in_col(1, 0, 0), in_col(-1, 0, 0), in_col(0, 1, 0), in_col(0, 0, 1)
    partner = in_row(1, 0)

    barrier = pltpu.get_barrier_semaphore()
    for k in range(1, 16):
        pl.semaphore_signal(barrier, inc=1, device_id=(row, (col + k) % 16), device_id_type=MESH)
    for k in range(1, 8):
        pl.semaphore_signal(barrier, inc=1, device_id=in_row(k // 4, k % 4), device_id_type=MESH)

    own = []
    for c in range(4):
        own.append(
            pltpu.make_async_copy(
                hidden.at[c], held.at[PLACE[(*OWN, c)] + core], load.at[c]
            )
        )
        own[c].start()
    load_weight = pltpu.make_async_copy(weight, keep, load.at[4])
    load_weight.start()
    load_teacher = pltpu.make_async_copy(teacher, whole, load.at[5])
    load_teacher.start()
    pl.semaphore_wait(barrier, 22)

    def chunks_of(step):
        first, count = STEPS[step]
        return [chunk for g in range(first, first + count) for chunk in GROUPS[g]]

    def chunk_at(chunk):
        if chunk[:2] == OWN:
            return hidden.at[chunk[2]]
        return held.at[PLACE[chunk] + core]

    def stream(plan, recv, device):
        return [
            remote(chunk_at(here), held.at[PLACE[there] + core], sent.at[0], recv.at[i], device)
            for i, (here, there) in enumerate(plan)
        ]

    ups = stream(SEND_UP, up_r, up)
    downs = stream(SEND_DOWN, down_r, down)
    sides = stream(SEND_SIDE, side_r, side)
    step_of = {chunk: s for s in range(steps) for chunk in chunks_of(s)}
    across = [
        remote(
            chunk_at(chunk), held.at[PLACE[chunk] + core], sent.at[0], core_r.at[step_of[chunk]], sibling
        )
        for chunk in ARRIVALS
    ]

    def arrived_bytes(ref, sem):
        pltpu.make_async_copy(ref, ref, sem).wait()

    def start_tick(tick):
        for copies, ticks in ((ups, START_UP), (downs, START_DOWN)):
            for copy, at in zip(copies, ticks):
                if at == tick:
                    copy.start()

    def start_side(tick):
        for copy, at in zip(sides, START_SIDE):
            if at == tick:
                copy.start()

    t_core, t_chunk, t_half = col // 8, (col % 8) // 2, col % 2
    t_place = (2 * t_core + t_half) * 4 + t_chunk
    t_cols = [
        remote(
            spread.at[(col + k) % 16],
            cols.at[t_place],
            sent.at[6],
            teacher_r.at[0],
            (row, (col + k) % 16),
        )
        for k in range(1, 16)
    ]
    t_own = pltpu.make_async_copy(spread.at[col], cols.at[t_place], load.at[5])
    t_rows = [
        remote(
            cols.at[pl.ds(((y + k % 4) % 4) * 4, 4)],
            targets.at[row],
            sent.at[7],
            teacher_r.at[1],
            in_row(k // 4, k % 4),
        )
        for k in range(1, 8)
    ]

    def quantize():
        load_weight.wait()
        span = 4 * TILE
        lane = lax.broadcasted_iota(jnp.int32, (8, span), 1)

        @pl.loop(0, depth // span)
        def _(i):
            ff = pl.ds(pl.multiple_of(i * span, span), span)
            for j in range(width // TILE):
                e = jnp.full((8, span), scale[j, 4 * i], jnp.int32)
                for k in range(1, 4):
                    e = jnp.where(lane < k * TILE, e, scale[j, 4 * i + k])
                step = (jnp.left_shift(jnp.int32(1), e + 14).astype(F32) * 2.0 ** (-14))[0:1]
                inverse = (jnp.left_shift(jnp.int32(1), -8 - e).astype(F32) * 256.0)[0:1]
                rows = slice(j * TILE, (j + 1) * TILE)
                levels = jnp.floor(keep[rows, ff].astype(F32) * inverse + 0.5)
                quant[rows, ff] = (jnp.clip(levels, -127.0, 127.0) * step).astype(BF16)
                keep[rows, ff] = (jnp.abs(levels) <= 127.0).astype(F32).astype(BF16)

    def part_copies(s):
        first, count = STEPS[s]
        return [
            remote(
                parts.at[(y + k) % 4, :, pl.ds(first, count)],
                got_y.at[k - 1, :, pl.ds(first, count)],
                sent.at[1],
                part_r.at[s],
                in_row(0, k),
            )
            for k in range(1, 4)
        ]

    def swap_copy(s):
        groups = pl.ds(*STEPS[s])
        return remote(swap.at[groups], got_x.at[groups], sent.at[2], swap_r.at[s], partner)

    def grad_copies(s):
        mine = grads.at[y, x_lo, pl.ds(*STEPS[s])]
        return [
            remote(mine, mine, sent.at[3], grad_y_r.at[s], in_row(0, k))
            for k in range(1, 4)
        ] + [remote(mine, mine, sent.at[4], grad_x_r.at[s], partner)]

    def forward_copies(s):
        theirs = grads.at[y, 1 - x_lo, pl.ds(*STEPS[s])]
        return [
            remote(theirs, theirs, sent.at[3], grad_y_r.at[s], in_row(0, k))
            for k in range(1, 4)
        ]

    def tokens_of(first, count, ff):
        return held[4 * first : 4 * (first + count), :, ff].reshape(4 * CHUNK * count, -1)

    def stage_a(s):
        first, count = STEPS[s]
        arrived_bytes(held.at[pl.ds(0, 2 * count)], core_r.at[s])

        part = lax.dot_general(
            quant[...], tokens_of(first, count, slice(None)), (((1,), (1,)), ((), ())),
            preferred_element_type=F32,
        ).T.astype(BF16)
        for g in range(count):
            for m in range(8):
                at = (g * 8 + m) * PIECE
                parts[m % 4, m // 4, first + g] = part[at : at + PIECE]

        for copy in last_parts() if s == steps - 1 else part_copies(s):
            copy.start()

    def last_parts():
        return [
            remote(
                parts.at[(y + k % 4) % 4, (x_lo + k // 4) % 2, last],
                got_last.at[k - 1],
                sent.at[5],
                last_r.at[0],
                in_row(k // 4, k % 4),
            )
            for k in range(1, 8)
        ]

    def last_grads():
        mine = grads.at[y, x_lo, last]
        return [
            remote(mine, mine, sent.at[5], last_r.at[1], in_row(k // 4, k % 4))
            for k in range(1, 8)
        ]

    def last_sum():
        arrived_bytes(got_last, last_r.at[0])
        student = parts[y, x_lo, last].astype(F32)
        for k in range(7):
            student = student + got_last[k].astype(F32)
        give(last, student)
        for copy in last_grads():
            copy.start()
        place(last)

    def over_y(x, g):
        value = parts[y, x, g].astype(F32)
        for k in range(3):
            value = value + got_y[k, x, g].astype(F32)
        return value

    def stage_b(s):
        first, count = STEPS[s]
        arrived_bytes(got_y.at[:, :, pl.ds(first, count)], part_r.at[s])
        for g in range(first, first + count):
            swap[g] = over_y(1 - x_lo, g).astype(BF16)
        swap_copy(s).start()

    def where_from(g):
        (dz0, p0, c0), (dz1, p1, c1) = GROUPS[g]
        t0 = ((z + dz0 + 4) % 4) * 2 + (x_hi + p0) % 2
        t1 = ((z + dz1 + 4) % 4) * 2 + (x_hi + p1) % 2
        return t0 + x_lo * (t1 - t0), c0 + x_lo * (c1 - c0)

    def piece_copy(g):
        t, c = where_from(g)
        spot = (y // 2) * 8 + 2 * c + y % 2
        return t, (
            pltpu.make_async_copy(pieces.at[g], placed.at[spot], out_r),
            remote(pieces.at[g], placed.at[spot], out_s.at[g], out_r, (t, col)),
        )

    def give(g, student):
        t, c = where_from(g)
        pieces[g] = student.astype(BF16)
        grads[y, x_lo, g] = ((student - targets[t, c].astype(F32)) * factor).astype(BF16)

    def place(g):
        t, (here, there) = piece_copy(g)

        @pl.when(t == row)
        def _():
            here.start()

        @pl.when(t != row)
        def _():
            there.start()

    def stage_c(s):
        swap_copy(s).wait_recv()
        first, count = STEPS[s]
        for g in range(first, first + count):
            give(g, over_y(x_lo, g) + got_x[g].astype(F32))
        for copy in grad_copies(s):
            copy.start()
        for g in range(first, first + count):
            place(g)

    def stage_d(s):
        grad_copies(s)[3].wait_recv()
        for copy in forward_copies(s):
            copy.start()

    def gradients(first, count):
        pieces_of = [grads[m % 4, m // 4, g] for g in range(first, first + count) for m in range(8)]
        return jnp.concatenate(pieces_of, axis=0).T

    def wait_gradients(s):
        if s == steps - 1:
            arrived_bytes(got_last, last_r.at[1])
        else:
            arrived_bytes(got_y.at[:, :, pl.ds(*STEPS[s])], grad_y_r.at[s])

    def stage_e(s, *more):
        for t in (s, *more):
            wait_gradients(t)
        first, count = STEPS[s]
        if s == 0:
            total[...] = jnp.dot(
                gradients(first, count), tokens_of(first, count, slice(None)), preferred_element_type=F32
            )
            return

        @pl.loop(0, 1 + len(more))
        def _(i):
            g = first + i * count
            pieces_of = [grads[m % 4, m // 4, g + k] for k in range(count) for m in range(8)]
            tokens = held[pl.ds(4 * g, 4 * count)].reshape(4 * CHUNK * count, depth)
            total[...] += jnp.dot(
                jnp.concatenate(pieces_of, axis=0).T, tokens, preferred_element_type=F32
            )

    def finish():
        for s in (steps - 2, steps - 1):
            wait_gradients(s)
        first = STEPS[steps - 2][0]
        count = len(GROUPS) - first
        g_t = gradients(first, count)
        span = depth // 4
        for i in range(4):
            ff = slice(i * span, (i + 1) * span)
            part = jnp.dot(g_t, tokens_of(first, count, ff), preferred_element_type=F32)
            grad[:, ff] = ((total[:, ff] + part) * keep[:, ff].astype(F32)).astype(BF16)
        arrived_bytes(placed, out_r)
        student_out[...] = placed[...].reshape(16 * PIECE, width).T

    stages = {"a": stage_a, "b": stage_b, "c": stage_c, "d": stage_d, "e": stage_e}

    start_tick(0)
    start_side(0)
    load_teacher.wait()
    for i in range(16):
        spread[i] = whole[:, i * width : (i + 1) * width]
    for copy in t_cols:
        copy.start()
    t_own.start()
    for c in range(4):
        across[c].start()

    for tick in range(11):
        if tick:
            arrived = [ups[tick - 1], downs[tick - 1]]
            names = [SEND_UP[tick - 1][1], SEND_DOWN[tick - 1][1]]
            for i, at in enumerate(ARRIVE_SIDE):
                if at == tick:
                    arrived.append(sides[i])
                    names.append(SEND_SIDE[i][1])
            for copy, name in zip(arrived, names):
                copy.wait_recv()
                across[NUMBER[name]].start()
            start_tick(tick)
        for what in PLAN[tick]:
            if what == "x":
                start_side(tick)
            elif what == "rows":
                t_own.wait()
                arrived_bytes(cols.at[pl.ds(0, 15)], teacher_r.at[0])
                for copy in t_rows:
                    copy.start()
                targets[row] = cols[pl.ds(y * 4, 4)]
            elif what == "targets":
                arrived_bytes(targets.at[pl.ds(0, 7)], teacher_r.at[1])
            elif what == "q":
                quantize()
                for copy in own:
                    copy.wait()
            elif what == "r":
                last_sum()
            elif what == "f":
                finish()
            else:
                stages[what[0]](*map(int, what[1:]))

    for g in range(16):
        t, (here, there) = piece_copy(g)

        @pl.when(t != row)
        def _():
            there.wait_send()

    sums = len(GROUPS) - 1
    for i, ref in enumerate((
        held.at[pl.ds(0, len(SEND_UP) + len(SEND_DOWN) + len(SEND_SIDE) + len(ARRIVALS))],
        got_y.at[:, :, pl.ds(0, sums)],
        swap.at[pl.ds(0, sums)],
        got_y.at[:, :, pl.ds(0, sums)],
        swap.at[pl.ds(0, sums)],
        swap.at[pl.ds(0, 14)],
        cols.at[pl.ds(0, 15)],
        targets.at[pl.ds(0, 7)],
    )):
        arrived_bytes(ref, sent.at[i])


def copy_out(student, grad, student_out, grad_out, sem):
    rows = grad.shape[0] // 6
    copies = [pltpu.make_async_copy(student, student_out, sem.at[6])]
    for i in range(6):
        part = pl.ds(i * rows, rows)
        copies.append(pltpu.make_async_copy(grad.at[part], grad_out.at[part], sem.at[i]))
    for copy in copies:
        copy.start()
    for copy in copies:
        copy.wait()


def local(hidden, weight, scale_exp, teacher):
    block, depth = hidden.shape
    width = weight.shape[1]
    tokens = block * lax.axis_size("col")
    groups, steps = len(GROUPS), len(STEPS)
    hidden = hidden.reshape(block // CHUNK, CHUNK, depth)
    dma = pltpu.SemaphoreType.DMA
    anywhere = pl.BlockSpec(memory_space=pl.ANY)
    student_out, grad = pl.pallas_call(
        functools.partial(kernel, 1.0 / math.sqrt(tokens)),
        out_shape=(
            pltpu.VMEM((width, 16 * PIECE), BF16),
            pltpu.VMEM((width, depth), BF16),
        ),
        in_specs=[anywhere, anywhere, pl.BlockSpec(memory_space=pltpu.SMEM), anywhere],
        out_specs=(pl.BlockSpec(memory_space=pltpu.VMEM),) * 2,
        scratch_shapes=[
            pltpu.VMEM((4 * groups, CHUNK, depth), BF16),
            pltpu.VMEM((width, depth), BF16),
            pltpu.VMEM((width, depth), BF16),
            pltpu.VMEM((width, depth), F32),
            pltpu.VMEM((16, depth), BF16),
            pltpu.VMEM((16, PIECE, width), BF16),
            pltpu.VMEM((4, 2, groups, PIECE, width), BF16),
            pltpu.VMEM((3, 2, groups, PIECE, width), BF16),
            pltpu.VMEM((groups, PIECE, width), BF16),
            pltpu.VMEM((groups, PIECE, width), BF16),
            pltpu.VMEM((7, PIECE, width), BF16),
            pltpu.VMEM((4, 2, groups, PIECE, width), BF16),
            pltpu.VMEM((groups, PIECE, width), BF16),
            pltpu.VMEM((16, PIECE, width), BF16),
            pltpu.VMEM((16, PIECE, width), BF16),
            pltpu.VMEM((8, 4, PIECE, width), BF16),
            dma((6,)), dma((8,)), dma((10,)), dma((10,)), dma((8,)), dma((steps,)),
            dma((steps,)), dma((steps,)), dma((steps,)), dma((steps,)), dma((groups,)), dma, dma((2,)), dma((2,)),
        ],
        compiler_params=pltpu.CompilerParams(
            collective_id=0, has_side_effects=True, vmem_limit_bytes=60 * 2**20
        ),
        cost_estimate=pl.CostEstimate(
            flops=4 * tokens * depth * width, bytes_accessed=3 * depth * width, transcendentals=0
        ),
    )(hidden, weight.T, scale_exp.T, teacher)
    student_out, grad = pl.pallas_call(
        copy_out,
        out_shape=tuple(jax.ShapeDtypeStruct(a.shape, a.dtype) for a in (student_out, grad)),
        in_specs=[pl.BlockSpec(memory_space=pltpu.VMEM)] * 2,
        out_specs=(anywhere, anywhere),
        scratch_shapes=[dma((7,))],
        compiler_params=pltpu.CompilerParams(vmem_limit_bytes=8 * 2**20),
    )(student_out, grad)
    return (student_out.T, grad.T)


def solution(mesh):
    placed = (P("col", "row"), P("row", "col"), P("row", "col"), P(("row", "col"), None))
    return jax.shard_map(
        local,
        mesh=mesh,
        in_specs=placed,
        out_specs=(P("row", "col"), P("row", "col")),
        check_vma=False,
    )
```

```python
import functools
import math

import jax
import jax.numpy as jnp
from jax import lax
from jax.experimental import pallas as pl
from jax.experimental.pallas import tpu as pltpu
from jax.sharding import PartitionSpec as P

MESH = pl.DeviceIdType.MESH
BF16, F32 = jnp.bfloat16, jnp.float32
TILE = 96
CHUNK = 32
PIECE = 16

OWN, DOWN, UP, FAR = (0, 0), (-1, 0), (1, 0), (2, 0)
SIDE, SIDE_DOWN, SIDE_UP, SIDE_FAR = (0, 1), (-1, 1), (1, 1), (2, 1)
GROUPS = (
    ((*OWN, 0), (*OWN, 1)),
    ((*OWN, 2), (*OWN, 3)),
    ((*DOWN, 0), (*UP, 2)),
    ((*DOWN, 1), (*UP, 3)),
    ((*SIDE, 0), (*SIDE, 1)),
    ((*SIDE, 2), (*SIDE, 3)),
    ((*FAR, 0), (*FAR, 2)),
    ((*FAR, 1), (*FAR, 3)),
    ((*DOWN, 2), (*UP, 0)),
    ((*DOWN, 3), (*UP, 1)),
    ((*SIDE_DOWN, 0), (*SIDE_UP, 0)),
    ((*SIDE_DOWN, 1), (*SIDE_UP, 1)),
    ((*SIDE_FAR, 0), (*SIDE_FAR, 2)),
    ((*SIDE_FAR, 1), (*SIDE_FAR, 3)),
    ((*SIDE_DOWN, 2), (*SIDE_UP, 2)),
    ((*SIDE_DOWN, 3), (*SIDE_UP, 3)),
)
PLACE = {chunk: 4 * g + 2 * j for g, pair in enumerate(GROUPS) for j, chunk in enumerate(pair)}
STEPS = ((0, 2), (2, 2), (4, 2), (6, 2), (8, 2), (10, 2), (12, 3), (15, 1))
DIRECT = 6
LATE = STEPS[DIRECT][0]
SEND_UP = [
    ((*OWN, 0), (*DOWN, 0)),
    ((*OWN, 1), (*DOWN, 1)),
    ((*DOWN, 0), (*FAR, 0)),
    ((*OWN, 2), (*DOWN, 2)),
    ((*DOWN, 1), (*FAR, 1)),
    ((*OWN, 3), (*DOWN, 3)),
] + [((*SIDE, c), (*SIDE_DOWN, c)) for c in range(4)]
SEND_DOWN = [
    ((*OWN, 2), (*UP, 2)),
    ((*OWN, 3), (*UP, 3)),
    ((*UP, 2), (*FAR, 2)),
    ((*OWN, 0), (*UP, 0)),
    ((*UP, 3), (*FAR, 3)),
    ((*OWN, 1), (*UP, 1)),
] + [((*SIDE, c), (*SIDE_UP, c)) for c in range(4)]
SEND_SIDE = [((*OWN, c), (*SIDE, c)) for c in range(4)] + [
    ((*FAR, c), (*SIDE_FAR, c)) for c in (0, 2, 1, 3)
]
START_UP = (0, 0, 1, 2, 3, 4, 5, 6, 7, 8)
START_DOWN = (0, 0, 1, 2, 3, 4, 5, 6, 7, 8)
START_SIDE = (-1, 0, 1, 2, 3, 4, 5, 6)
ARRIVE_SIDE = (2, 3, 4, 5, 6, 7, 8)
ARRIVALS = (
    [(*OWN, c) for c in range(4)]
    + [there for _, there in SEND_UP]
    + [there for _, there in SEND_DOWN]
    + [there for _, there in SEND_SIDE]
)
NUMBER = {chunk: i for i, chunk in enumerate(ARRIVALS)}
PLAN = (
    ("q", "a0", "x",),
    ("x",),
    ("rows", "b0", "x", "a1",),
    ("x",),
    ("targets", "c0", "b1", "x",),
    ("c1", "x", "a3", "a2",),
    ("x", "a4", "b3", "b2",),
    ("d0", "d1", "b4",),
    ("e0", "e1", "a5",),
    ("c3", "c2", "c4", "w", "b5", "d3", "d2", "a6", "c5", "d4",),
    ("a7", "d5", "e23", "r6", "r7", "e45", "f",),
)


def kernel(
    factor,
    hidden, weight, scale, teacher,
    student_out, grad,
    held, keep, quant, total, whole, spread, parts, got_y, swap, got_x, got_late, grads, pieces, placed, cols, targets,
    load, sent, up_r, down_r, side_r, core_r, part_r, swap_r, grad_y_r, grad_x_r, out_s, out_r, late_r, teacher_r,
):
    row, col = lax.axis_index("row"), lax.axis_index("col")
    x_lo, y = row // 4, row % 4
    z, x_hi, core = col // 4, (col // 2) % 2, col % 2
    width = grad.shape[0]
    depth = held.shape[-1]
    steps = len(STEPS)

    def piece(value):
        return value[..., :width].astype(F32)

    def padded(value):
        spare = parts.shape[-1] - width
        return jnp.concatenate([value, jnp.zeros((value.shape[0], spare), F32)], axis=1).astype(BF16)

    def in_col(dz, p, dc):
        return (row, ((z + dz + 4) % 4) * 4 + ((x_hi + p) % 2) * 2 + (core + dc) % 2)

    def in_row(dx, dy):
        return (((x_lo + dx) % 2) * 4 + (y + dy) % 4, col)

    def remote(src, dst, send, recv, device):
        return pltpu.make_async_remote_copy(
            src_ref=src, dst_ref=dst, send_sem=send, recv_sem=recv, device_id=device, device_id_type=MESH
        )

    up, down, side, sibling = in_col(1, 0, 0), in_col(-1, 0, 0), in_col(0, 1, 0), in_col(0, 0, 1)
    partner = in_row(1, 0)

    load_teacher = pltpu.make_async_copy(teacher, whole, load.at[5])
    load_teacher.start()
    barrier = pltpu.get_barrier_semaphore()
    for k in range(1, 16):
        pl.semaphore_signal(barrier, inc=1, device_id=(row, (col + k) % 16), device_id_type=MESH)
    for k in range(1, 8):
        pl.semaphore_signal(barrier, inc=1, device_id=in_row(k // 4, k % 4), device_id_type=MESH)

    own = []
    for c in range(4):
        own.append(
            pltpu.make_async_copy(
                hidden.at[c], held.at[PLACE[(*OWN, c)] + core], load.at[c]
            )
        )
        own[c].start()
    load_weight = pltpu.make_async_copy(weight, keep, load.at[4])
    load_weight.start()
    load_teacher.wait()
    for i in range(16):
        spread[i] = padded(whole[:, i * width : (i + 1) * width].astype(F32))
    pl.semaphore_wait(barrier, 22)

    def chunks_of(step):
        first, count = STEPS[step]
        return [chunk for g in range(first, first + count) for chunk in GROUPS[g]]

    def chunk_at(chunk):
        if chunk[:2] == OWN:
            return hidden.at[chunk[2]]
        return held.at[PLACE[chunk] + core]

    def stream(plan, recv, device):
        return [
            remote(chunk_at(here), held.at[PLACE[there] + core], sent.at[0], recv.at[i], device)
            for i, (here, there) in enumerate(plan)
        ]

    ups = stream(SEND_UP, up_r, up)
    downs = stream(SEND_DOWN, down_r, down)
    sides = stream(SEND_SIDE, side_r, side)
    step_of = {chunk: s for s in range(steps) for chunk in chunks_of(s)}
    across = [
        remote(
            chunk_at(chunk), held.at[PLACE[chunk] + core], sent.at[0], core_r.at[step_of[chunk]], sibling
        )
        for chunk in ARRIVALS
    ]

    def arrived_bytes(ref, sem):
        pltpu.make_async_copy(ref, ref, sem).wait()

    def start_tick(tick):
        for copies, ticks in ((ups, START_UP), (downs, START_DOWN)):
            for copy, at in zip(copies, ticks):
                if at == tick:
                    copy.start()

    def start_side(tick):
        for copy, at in zip(sides, START_SIDE):
            if at == tick:
                copy.start()

    t_core, t_chunk, t_half = col // 8, (col % 8) // 2, col % 2
    t_place = (2 * t_core + t_half) * 4 + t_chunk
    t_cols = [
        remote(
            spread.at[(col + k) % 16],
            cols.at[t_place],
            sent.at[6],
            teacher_r.at[0],
            (row, (col + k) % 16),
        )
        for k in range(1, 16)
    ]
    t_own = pltpu.make_async_copy(spread.at[col], cols.at[t_place], load.at[5])
    t_rows = [
        remote(
            cols.at[pl.ds(((y + k % 4) % 4) * 4, 4)],
            targets.at[row],
            sent.at[7],
            teacher_r.at[1],
            in_row(k // 4, k % 4),
        )
        for k in range(1, 8)
    ]

    def quantize():
        load_weight.wait()
        span = 4 * TILE
        lane = lax.broadcasted_iota(jnp.int32, (8, span), 1)

        @pl.loop(0, depth // span)
        def _(i):
            ff = pl.ds(pl.multiple_of(i * span, span), span)
            for j in range(width // TILE):
                e = jnp.full((8, span), scale[j, 4 * i], jnp.int32)
                for k in range(1, 4):
                    e = jnp.where(lane < k * TILE, e, scale[j, 4 * i + k])
                step = (jnp.left_shift(jnp.int32(1), e + 14).astype(F32) * 2.0 ** (-14))[0:1]
                inverse = (jnp.left_shift(jnp.int32(1), -8 - e).astype(F32) * 256.0)[0:1]
                rows = slice(j * TILE, (j + 1) * TILE)
                levels = jnp.floor(keep[rows, ff].astype(F32) * inverse + 0.5)
                quant[rows, ff] = (jnp.clip(levels, -127.0, 127.0) * step).astype(BF16)
                keep[rows, ff] = (jnp.abs(levels) <= 127.0).astype(F32).astype(BF16)

    def part_copies(s):
        first, count = STEPS[s]
        return [
            remote(
                parts.at[(y + k) % 4, :, pl.ds(first, count)],
                got_y.at[k - 1, :, pl.ds(first, count)],
                sent.at[1],
                part_r.at[s],
                in_row(0, k),
            )
            for k in range(1, 4)
        ]

    def swap_copy(s):
        groups = pl.ds(*STEPS[s])
        return remote(swap.at[groups], got_x.at[groups], sent.at[2], swap_r.at[s], partner)

    def grad_copies(s):
        mine = grads.at[y, x_lo, pl.ds(*STEPS[s])]
        return [
            remote(mine, mine, sent.at[3], grad_y_r.at[s], in_row(0, k))
            for k in range(1, 4)
        ] + [remote(mine, mine, sent.at[4], grad_x_r.at[s], partner)]

    def forward_copies(s):
        theirs = grads.at[y, 1 - x_lo, pl.ds(*STEPS[s])]
        return [
            remote(theirs, theirs, sent.at[3], grad_y_r.at[s], in_row(0, k))
            for k in range(1, 4)
        ]

    def tokens_of(first, count, ff):
        return held[4 * first : 4 * (first + count), :, ff].reshape(4 * CHUNK * count, -1)

    def stage_a(s):
        first, count = STEPS[s]
        arrived_bytes(held.at[pl.ds(0, 2 * count)], core_r.at[s])

        part = lax.dot_general(
            quant[...], tokens_of(first, count, slice(None)), (((1,), (1,)), ((), ())),
            preferred_element_type=F32,
        ).T
        part = padded(part)
        for g in range(count):
            for m in range(8):
                at = (g * 8 + m) * PIECE
                parts[m % 4, m // 4, first + g] = part[at : at + PIECE]

        for copy in direct_parts(s) if s >= DIRECT else part_copies(s):
            copy.start()

    def direct_parts(s):
        first, count = STEPS[s]
        return [
            remote(
                parts.at[(y + k % 4) % 4, (x_lo + k // 4) % 2, pl.ds(first, count)],
                got_late.at[k - 1, pl.ds(first - LATE, count)],
                sent.at[5],
                late_r.at[0, s - DIRECT],
                in_row(k // 4, k % 4),
            )
            for k in range(1, 8)
        ]

    def direct_grads(s):
        mine = grads.at[y, x_lo, pl.ds(*STEPS[s])]
        return [
            remote(mine, mine, sent.at[8], late_r.at[1, s - DIRECT], in_row(k // 4, k % 4))
            for k in range(1, 8)
        ]

    def late_bytes(s):
        first, count = STEPS[s]
        return got_late.at[:, pl.ds(first - LATE, count)]

    def stage_r(s):
        arrived_bytes(late_bytes(s), late_r.at[0, s - DIRECT])
        first, count = STEPS[s]
        for g in range(first, first + count):
            student = piece(parts[y, x_lo, g])
            for k in range(7):
                student = student + piece(got_late[k, g - LATE])
            give(g, student)
        for copy in direct_grads(s):
            copy.start()
        for g in range(first, first + count):
            place(g)

    def over_y(x, g):
        value = piece(parts[y, x, g])
        for k in range(3):
            value = value + piece(got_y[k, x, g])
        return value

    def stage_b(s):
        first, count = STEPS[s]
        arrived_bytes(got_y.at[:, :, pl.ds(first, count)], part_r.at[s])
        for g in range(first, first + count):
            swap[g] = padded(over_y(1 - x_lo, g))
        swap_copy(s).start()

    def where_from(g):
        (dz0, p0, c0), (dz1, p1, c1) = GROUPS[g]
        t0 = ((z + dz0 + 4) % 4) * 2 + (x_hi + p0) % 2
        t1 = ((z + dz1 + 4) % 4) * 2 + (x_hi + p1) % 2
        return t0 + x_lo * (t1 - t0), c0 + x_lo * (c1 - c0)

    def piece_copy(g):
        t, c = where_from(g)
        spot = (y // 2) * 8 + 2 * c + y % 2
        return t, (
            pltpu.make_async_copy(pieces.at[g], placed.at[spot], out_r),
            remote(pieces.at[g], placed.at[spot], out_s.at[g], out_r, (t, col)),
        )

    def give(g, student):
        t, c = where_from(g)
        pieces[g] = padded(student)
        grads[y, x_lo, g] = padded((student - piece(targets[t, c])) * factor)

    def place(g):
        t, (here, there) = piece_copy(g)

        @pl.when(t == row)
        def _():
            here.start()

        @pl.when(t != row)
        def _():
            there.start()

    def stage_c(s):
        swap_copy(s).wait_recv()
        first, count = STEPS[s]
        for g in range(first, first + count):
            give(g, over_y(x_lo, g) + piece(got_x[g]))
        for copy in grad_copies(s):
            copy.start()
        for g in range(first, first + count):
            place(g)

    def stage_d(s):
        grad_copies(s)[3].wait_recv()
        for copy in forward_copies(s):
            copy.start()

    def gradients(first, count):
        pieces_of = [grads[m % 4, m // 4, g] for g in range(first, first + count) for m in range(8)]
        return jnp.concatenate(pieces_of, axis=0)[:, :width].T

    def wait_gradients(s):
        if s >= DIRECT:
            arrived_bytes(late_bytes(s), late_r.at[1, s - DIRECT])
        else:
            arrived_bytes(got_y.at[:, :, pl.ds(*STEPS[s])], grad_y_r.at[s])

    def stage_e(s, *more):
        for t in (s, *more):
            wait_gradients(t)
        first, count = STEPS[s]
        if s == 0:
            total[...] = jnp.dot(
                gradients(first, count), tokens_of(first, count, slice(None)), preferred_element_type=F32
            )
            return

        @pl.loop(0, 1 + len(more))
        def _(i):
            g = first + i * count
            pieces_of = [grads[m % 4, m // 4, g + k] for k in range(count) for m in range(8)]
            tokens = held[pl.ds(4 * g, 4 * count)].reshape(4 * CHUNK * count, depth)
            total[...] += jnp.dot(
                jnp.concatenate(pieces_of, axis=0)[:, :width].T, tokens, preferred_element_type=F32
            )

    def finish():
        for s in (steps - 2, steps - 1):
            wait_gradients(s)
        first = STEPS[steps - 2][0]
        count = len(GROUPS) - first
        g_t = gradients(first, count)
        span = depth // 4
        for i in range(4):
            ff = slice(i * span, (i + 1) * span)
            part = jnp.dot(g_t, tokens_of(first, count, ff), preferred_element_type=F32)
            grad[:, ff] = ((total[:, ff] + part) * keep[:, ff].astype(F32)).astype(BF16)
        arrived_bytes(placed, out_r)
        student_out[...] = placed[...].reshape(16 * PIECE, -1)[:, :width].T

    stages = {"a": stage_a, "r": stage_r, "b": stage_b, "c": stage_c, "d": stage_d, "e": stage_e}

    for copy in t_cols:
        copy.start()
    start_tick(0)
    start_side(-1)
    t_own.start()
    for c in range(4):
        across[c].start()

    for tick in range(11):
        if tick:
            arrived = [ups[tick - 1], downs[tick - 1]]
            names = [SEND_UP[tick - 1][1], SEND_DOWN[tick - 1][1]]
            for i, at in enumerate(ARRIVE_SIDE):
                if at == tick:
                    arrived.append(sides[i])
                    names.append(SEND_SIDE[i][1])
            for copy, name in zip(arrived, names):
                copy.wait_recv()
                across[NUMBER[name]].start()
            start_tick(tick)
        for what in PLAN[tick]:
            if what == "x":
                start_side(tick)
            elif what == "w":
                sides[-1].wait_recv()
                across[-1].start()
            elif what == "rows":
                t_own.wait()
                arrived_bytes(cols.at[pl.ds(0, 15)], teacher_r.at[0])
                for copy in t_rows:
                    copy.start()
                targets[row] = cols[pl.ds(y * 4, 4)]
            elif what == "targets":
                arrived_bytes(targets.at[pl.ds(0, 7)], teacher_r.at[1])
            elif what == "q":
                quantize()
                for copy in own:
                    copy.wait()
            elif what == "f":
                finish()
            else:
                stages[what[0]](*map(int, what[1:]))

    for g in range(16):
        t, (here, there) = piece_copy(g)

        @pl.when(t != row)
        def _():
            there.wait_send()

    sums = LATE
    for i, ref in enumerate((
        held.at[pl.ds(0, len(SEND_UP) + len(SEND_DOWN) + len(SEND_SIDE) + len(ARRIVALS))],
        got_y.at[:, :, pl.ds(0, sums)],
        swap.at[pl.ds(0, sums)],
        got_y.at[:, :, pl.ds(0, sums)],
        swap.at[pl.ds(0, sums)],
        got_late,
        cols.at[pl.ds(0, 15)],
        targets.at[pl.ds(0, 7)],
        got_late,
    )):
        arrived_bytes(ref, sent.at[i])


def copy_out(student, grad, student_out, grad_out, sem):
    rows = grad.shape[0] // 6
    copies = [pltpu.make_async_copy(student, student_out, sem.at[6])]
    for i in range(6):
        part = pl.ds(i * rows, rows)
        copies.append(pltpu.make_async_copy(grad.at[part], grad_out.at[part], sem.at[i]))
    for copy in copies:
        copy.start()
    for copy in copies:
        copy.wait()


def local(hidden, weight, scale_exp, teacher):
    block, depth = hidden.shape
    width = weight.shape[1]
    tokens = block * lax.axis_size("col")
    groups, steps = len(GROUPS), len(STEPS)
    wide = -(-width // 128) * 128
    hidden = hidden.reshape(block // CHUNK, CHUNK, depth)
    dma = pltpu.SemaphoreType.DMA
    anywhere = pl.BlockSpec(memory_space=pl.ANY)
    student_out, grad = pl.pallas_call(
        functools.partial(kernel, 1.0 / math.sqrt(tokens)),
        out_shape=(
            pltpu.VMEM((width, 16 * PIECE), BF16),
            pltpu.VMEM((width, depth), BF16),
        ),
        in_specs=[anywhere, anywhere, pl.BlockSpec(memory_space=pltpu.SMEM), anywhere],
        out_specs=(pl.BlockSpec(memory_space=pltpu.VMEM),) * 2,
        scratch_shapes=[
            pltpu.VMEM((4 * groups, CHUNK, depth), BF16),
            pltpu.VMEM((width, depth), BF16),
            pltpu.VMEM((width, depth), BF16),
            pltpu.VMEM((width, depth), F32),
            pltpu.VMEM((16, depth), BF16),
            pltpu.VMEM((16, PIECE, wide), BF16),
            pltpu.VMEM((4, 2, groups, PIECE, wide), BF16),
            pltpu.VMEM((3, 2, groups, PIECE, wide), BF16),
            pltpu.VMEM((groups, PIECE, wide), BF16),
            pltpu.VMEM((groups, PIECE, wide), BF16),
            pltpu.VMEM((7, groups - LATE, PIECE, wide), BF16),
            pltpu.VMEM((4, 2, groups, PIECE, wide), BF16),
            pltpu.VMEM((groups, PIECE, wide), BF16),
            pltpu.VMEM((16, PIECE, wide), BF16),
            pltpu.VMEM((16, PIECE, wide), BF16),
            pltpu.VMEM((8, 4, PIECE, wide), BF16),
            dma((6,)), dma((9,)), dma((10,)), dma((10,)), dma((8,)), dma((steps,)),
            dma((steps,)), dma((steps,)), dma((steps,)), dma((steps,)), dma((groups,)), dma, dma((2, steps - DIRECT)), dma((2,)),
        ],
        compiler_params=pltpu.CompilerParams(
            collective_id=0, has_side_effects=True, vmem_limit_bytes=60 * 2**20
        ),
        cost_estimate=pl.CostEstimate(
            flops=4 * tokens * depth * width, bytes_accessed=3 * depth * width, transcendentals=0
        ),
    )(hidden, weight.T, scale_exp.T, teacher)
    student_out, grad = pl.pallas_call(
        copy_out,
        out_shape=tuple(jax.ShapeDtypeStruct(a.shape, a.dtype) for a in (student_out, grad)),
        in_specs=[pl.BlockSpec(memory_space=pltpu.VMEM)] * 2,
        out_specs=(anywhere, anywhere),
        scratch_shapes=[dma((7,))],
        compiler_params=pltpu.CompilerParams(vmem_limit_bytes=8 * 2**20),
    )(student_out, grad)
    return (student_out.T, grad.T)


def solution(mesh):
    placed = (P("col", "row"), P("row", "col"), P("row", "col"), P(("row", "col"), None))
    return jax.shard_map(
        local,
        mesh=mesh,
        in_specs=placed,
        out_specs=(P("row", "col"), P("row", "col")),
        check_vma=False,
    )
```

```python
import functools
import math

import jax
import jax.numpy as jnp
from jax import lax
from jax.experimental import pallas as pl
from jax.experimental.pallas import tpu as pltpu
from jax.sharding import PartitionSpec as P

MESH = pl.DeviceIdType.MESH
BF16, F32 = jnp.bfloat16, jnp.float32
TILE = 96
CHUNK = 32
PIECE = 16

OWN, DOWN, UP, FAR = (0, 0), (-1, 0), (1, 0), (2, 0)
SIDE, SIDE_DOWN, SIDE_UP, SIDE_FAR = (0, 1), (-1, 1), (1, 1), (2, 1)
GROUPS = (
    ((*OWN, 0), (*OWN, 1)),
    ((*OWN, 2), (*OWN, 3)),
    ((*DOWN, 0), (*UP, 2)),
    ((*DOWN, 1), (*UP, 3)),
    ((*SIDE, 0), (*SIDE, 1)),
    ((*SIDE, 2), (*SIDE, 3)),
    ((*FAR, 0), (*FAR, 2)),
    ((*FAR, 1), (*FAR, 3)),
    ((*DOWN, 2), (*UP, 0)),
    ((*DOWN, 3), (*UP, 1)),
    ((*SIDE_DOWN, 0), (*SIDE_UP, 0)),
    ((*SIDE_DOWN, 1), (*SIDE_UP, 1)),
    ((*SIDE_FAR, 0), (*SIDE_FAR, 2)),
    ((*SIDE_FAR, 1), (*SIDE_FAR, 3)),
    ((*SIDE_DOWN, 2), (*SIDE_UP, 2)),
    ((*SIDE_DOWN, 3), (*SIDE_UP, 3)),
)
PLACE = {chunk: 4 * g + 2 * j for g, pair in enumerate(GROUPS) for j, chunk in enumerate(pair)}
STEPS = ((0, 2), (2, 2), (4, 2), (6, 2), (8, 2), (10, 2), (12, 3), (15, 1))
DIRECT = 7
LATE = STEPS[DIRECT][0]
SEND_UP = [
    ((*OWN, 0), (*DOWN, 0)),
    ((*OWN, 1), (*DOWN, 1)),
    ((*DOWN, 0), (*FAR, 0)),
    ((*OWN, 2), (*DOWN, 2)),
    ((*DOWN, 1), (*FAR, 1)),
    ((*OWN, 3), (*DOWN, 3)),
] + [((*SIDE, c), (*SIDE_DOWN, c)) for c in range(4)]
SEND_DOWN = [
    ((*OWN, 2), (*UP, 2)),
    ((*OWN, 3), (*UP, 3)),
    ((*UP, 2), (*FAR, 2)),
    ((*OWN, 0), (*UP, 0)),
    ((*UP, 3), (*FAR, 3)),
    ((*OWN, 1), (*UP, 1)),
] + [((*SIDE, c), (*SIDE_UP, c)) for c in range(4)]
SEND_SIDE = [((*OWN, c), (*SIDE, c)) for c in range(4)] + [
    ((*FAR, c), (*SIDE_FAR, c)) for c in (0, 2, 1, 3)
]
START_UP = (0, 0, 1, 2, 3, 4, 5, 6, 7, 8)
START_DOWN = (0, 0, 1, 2, 3, 4, 5, 6, 7, 8)
START_SIDE = (-1, 0, 1, 2, 3, 4, 5, 6)
ARRIVE_SIDE = (2, 3, 4, 5, 6, 7, 8)
ARRIVALS = (
    [(*OWN, c) for c in range(4)]
    + [there for _, there in SEND_UP]
    + [there for _, there in SEND_DOWN]
    + [there for _, there in SEND_SIDE]
)
NUMBER = {chunk: i for i, chunk in enumerate(ARRIVALS)}
PLAN = (
    ("q", "a0", "x",),
    ("x",),
    ("rows", "b0", "x", "a1",),
    ("x",),
    ("targets", "c0", "b1", "x",),
    ("c1", "x", "a3", "a2",),
    ("a4", "b3", "b2", "x",),
    ("d0", "d1", "b4",),
    ("c3", "c2", "e0", "a5", "e1",),
    ("c4", "d3", "d2", "w", "a6", "b5", "d4",),
    ("a7", "c5", "b6", "d5", "c6", "r7", "e23", "d6", "e45", "f",),
)


def kernel(
    factor,
    hidden, weight, scale, teacher,
    student_out, grad,
    held, keep, quant, total, whole, spread, parts, got_y, swap, got_x, got_late, grads, pieces, placed, cols, targets,
    load, sent, up_r, down_r, side_r, core_r, part_r, swap_r, grad_y_r, grad_x_r, out_s, out_r, late_r, teacher_r,
):
    row, col = lax.axis_index("row"), lax.axis_index("col")
    x_lo, y = row // 4, row % 4
    z, x_hi, core = col // 4, (col // 2) % 2, col % 2
    width = grad.shape[0]
    depth = held.shape[-1]
    steps = len(STEPS)

    def piece(value):
        return value.astype(F32)

    def rounded(value):
        return value.astype(BF16)

    def in_col(dz, p, dc):
        return (row, ((z + dz + 4) % 4) * 4 + ((x_hi + p) % 2) * 2 + (core + dc) % 2)

    def in_row(dx, dy):
        return (((x_lo + dx) % 2) * 4 + (y + dy) % 4, col)

    def remote(src, dst, send, recv, device):
        return pltpu.make_async_remote_copy(
            src_ref=src, dst_ref=dst, send_sem=send, recv_sem=recv, device_id=device, device_id_type=MESH
        )

    up, down, side, sibling = in_col(1, 0, 0), in_col(-1, 0, 0), in_col(0, 1, 0), in_col(0, 0, 1)
    partner = in_row(1, 0)

    load_teacher = pltpu.make_async_copy(teacher, whole, load.at[5])
    load_teacher.start()
    barrier = pltpu.get_barrier_semaphore()
    for k in range(1, 16):
        pl.semaphore_signal(barrier, inc=1, device_id=(row, (col + k) % 16), device_id_type=MESH)
    for k in range(1, 8):
        pl.semaphore_signal(barrier, inc=1, device_id=in_row(k // 4, k % 4), device_id_type=MESH)

    own = []
    for c in range(4):
        own.append(
            pltpu.make_async_copy(
                hidden.at[c], held.at[PLACE[(*OWN, c)] + core], load.at[c]
            )
        )
        own[c].start()
    load_weight = pltpu.make_async_copy(weight, keep, load.at[4])
    load_weight.start()
    load_teacher.wait()
    for i in range(16):
        spread[i] = whole[:, i * width : (i + 1) * width]
    pl.semaphore_wait(barrier, 22)

    def chunks_of(step):
        first, count = STEPS[step]
        return [chunk for g in range(first, first + count) for chunk in GROUPS[g]]

    def chunk_at(chunk):
        if chunk[:2] == OWN:
            return hidden.at[chunk[2]]
        return held.at[PLACE[chunk] + core]

    def stream(plan, recv, device):
        return [
            remote(chunk_at(here), held.at[PLACE[there] + core], sent.at[0], recv.at[i], device)
            for i, (here, there) in enumerate(plan)
        ]

    ups = stream(SEND_UP, up_r, up)
    downs = stream(SEND_DOWN, down_r, down)
    sides = stream(SEND_SIDE, side_r, side)
    step_of = {chunk: s for s in range(steps) for chunk in chunks_of(s)}
    across = [
        remote(
            chunk_at(chunk), held.at[PLACE[chunk] + core], sent.at[0], core_r.at[step_of[chunk]], sibling
        )
        for chunk in ARRIVALS
    ]

    def arrived_bytes(ref, sem):
        pltpu.make_async_copy(ref, ref, sem).wait()

    def start_tick(tick):
        for copies, ticks in ((ups, START_UP), (downs, START_DOWN)):
            for copy, at in zip(copies, ticks):
                if at == tick:
                    copy.start()

    def start_side(tick):
        for copy, at in zip(sides, START_SIDE):
            if at == tick:
                copy.start()

    t_core, t_chunk, t_half = col // 8, (col % 8) // 2, col % 2
    t_place = (2 * t_core + t_half) * 4 + t_chunk
    t_cols = [
        remote(
            spread.at[(col + k) % 16],
            cols.at[t_place],
            sent.at[6],
            teacher_r.at[0],
            (row, (col + k) % 16),
        )
        for k in range(1, 16)
    ]
    t_own = pltpu.make_async_copy(spread.at[col], cols.at[t_place], load.at[5])
    t_rows = [
        remote(
            cols.at[pl.ds(((y + k % 4) % 4) * 4, 4)],
            targets.at[row],
            sent.at[7],
            teacher_r.at[1],
            in_row(k // 4, k % 4),
        )
        for k in range(1, 8)
    ]

    def quantize():
        load_weight.wait()
        span = 4 * TILE
        lane = lax.broadcasted_iota(jnp.int32, (8, span), 1)

        @pl.loop(0, depth // span)
        def _(i):
            ff = pl.ds(pl.multiple_of(i * span, span), span)
            for j in range(width // TILE):
                e = jnp.full((8, span), scale[j, 4 * i], jnp.int32)
                for k in range(1, 4):
                    e = jnp.where(lane < k * TILE, e, scale[j, 4 * i + k])
                step = (jnp.left_shift(jnp.int32(1), e + 14).astype(F32) * 2.0 ** (-14))[0:1]
                inverse = (jnp.left_shift(jnp.int32(1), -8 - e).astype(F32) * 256.0)[0:1]
                rows = slice(j * TILE, (j + 1) * TILE)
                levels = jnp.floor(keep[rows, ff].astype(F32) * inverse + 0.5)
                quant[rows, ff] = (jnp.clip(levels, -127.0, 127.0) * step).astype(BF16)
                keep[rows, ff] = (jnp.abs(levels) <= 127.0).astype(F32).astype(BF16)

    def part_copies(s):
        first, count = STEPS[s]
        return [
            remote(
                parts.at[(y + k) % 4, :, pl.ds(first, count)],
                got_y.at[k - 1, :, pl.ds(first, count)],
                sent.at[1],
                part_r.at[s],
                in_row(0, k),
            )
            for k in range(1, 4)
        ]

    def swap_copy(s):
        groups = pl.ds(*STEPS[s])
        return remote(swap.at[groups], got_x.at[groups], sent.at[2], swap_r.at[s], partner)

    def grad_copies(s):
        mine = grads.at[y, x_lo, pl.ds(*STEPS[s])]
        return [
            remote(mine, mine, sent.at[3], grad_y_r.at[s], in_row(0, k))
            for k in range(1, 4)
        ] + [remote(mine, mine, sent.at[4], grad_x_r.at[s], partner)]

    def forward_copies(s):
        theirs = grads.at[y, 1 - x_lo, pl.ds(*STEPS[s])]
        return [
            remote(theirs, theirs, sent.at[3], grad_y_r.at[s], in_row(0, k))
            for k in range(1, 4)
        ]

    def tokens_of(first, count, ff):
        return held[4 * first : 4 * (first + count), :, ff].reshape(4 * CHUNK * count, -1)

    def stage_a(s):
        first, count = STEPS[s]
        arrived_bytes(held.at[pl.ds(0, 2 * count)], core_r.at[s])

        part = lax.dot_general(
            quant[...], tokens_of(first, count, slice(None)), (((1,), (1,)), ((), ())),
            preferred_element_type=F32,
        ).T
        part = rounded(part)
        for g in range(count):
            for m in range(8):
                at = (g * 8 + m) * PIECE
                parts[m % 4, m // 4, first + g] = part[at : at + PIECE]

        for copy in direct_parts(s) if s >= DIRECT else part_copies(s):
            copy.start()

    def direct_parts(s):
        first, count = STEPS[s]
        return [
            remote(
                parts.at[(y + k % 4) % 4, (x_lo + k // 4) % 2, pl.ds(first, count)],
                got_late.at[k - 1, pl.ds(first - LATE, count)],
                sent.at[5],
                late_r.at[0, s - DIRECT],
                in_row(k // 4, k % 4),
            )
            for k in range(1, 8)
        ]

    def direct_grads(s):
        mine = grads.at[y, x_lo, pl.ds(*STEPS[s])]
        return [
            remote(mine, mine, sent.at[8], late_r.at[1, s - DIRECT], in_row(k // 4, k % 4))
            for k in range(1, 8)
        ]

    def late_bytes(s):
        first, count = STEPS[s]
        return got_late.at[:, pl.ds(first - LATE, count)]

    def stage_r(s):
        arrived_bytes(late_bytes(s), late_r.at[0, s - DIRECT])
        first, count = STEPS[s]
        for g in range(first, first + count):
            student = piece(parts[y, x_lo, g])
            for k in range(7):
                student = student + piece(got_late[k, g - LATE])
            give(g, student)
        for copy in direct_grads(s):
            copy.start()
        for g in range(first, first + count):
            place(g)

    def over_y(x, g):
        value = piece(parts[y, x, g])
        for k in range(3):
            value = value + piece(got_y[k, x, g])
        return value

    def stage_b(s):
        first, count = STEPS[s]
        arrived_bytes(got_y.at[:, :, pl.ds(first, count)], part_r.at[s])
        for g in range(first, first + count):
            swap[g] = rounded(over_y(1 - x_lo, g))
        swap_copy(s).start()

    def where_from(g):
        (dz0, p0, c0), (dz1, p1, c1) = GROUPS[g]
        t0 = ((z + dz0 + 4) % 4) * 2 + (x_hi + p0) % 2
        t1 = ((z + dz1 + 4) % 4) * 2 + (x_hi + p1) % 2
        return t0 + x_lo * (t1 - t0), c0 + x_lo * (c1 - c0)

    def piece_copy(g):
        t, c = where_from(g)
        spot = (y // 2) * 8 + 2 * c + y % 2
        return t, (
            pltpu.make_async_copy(pieces.at[g], placed.at[spot], out_r),
            remote(pieces.at[g], placed.at[spot], out_s.at[g], out_r, (t, col)),
        )

    def give(g, student):
        t, c = where_from(g)
        pieces[g] = rounded(student)
        grads[y, x_lo, g] = rounded((student - piece(targets[t, c])) * factor)

    def place(g):
        t, (here, there) = piece_copy(g)

        @pl.when(t == row)
        def _():
            here.start()

        @pl.when(t != row)
        def _():
            there.start()

    def stage_c(s):
        swap_copy(s).wait_recv()
        first, count = STEPS[s]
        for g in range(first, first + count):
            give(g, over_y(x_lo, g) + piece(got_x[g]))
        for copy in grad_copies(s):
            copy.start()
        for g in range(first, first + count):
            place(g)

    def stage_d(s):
        grad_copies(s)[3].wait_recv()
        for copy in forward_copies(s):
            copy.start()

    def gradients(first, count):
        pieces_of = [grads[m % 4, m // 4, g] for g in range(first, first + count) for m in range(8)]
        return jnp.concatenate(pieces_of, axis=0).T

    def wait_gradients(s):
        if s >= DIRECT:
            arrived_bytes(late_bytes(s), late_r.at[1, s - DIRECT])
        else:
            arrived_bytes(got_y.at[:, :, pl.ds(*STEPS[s])], grad_y_r.at[s])

    def stage_e(s, *more):
        for t in (s, *more):
            wait_gradients(t)
        first, count = STEPS[s]
        if s == 0:
            total[...] = jnp.dot(
                gradients(first, count), tokens_of(first, count, slice(None)), preferred_element_type=F32
            )
            return

        @pl.loop(0, 1 + len(more))
        def _(i):
            g = first + i * count
            pieces_of = [grads[m % 4, m // 4, g + k] for k in range(count) for m in range(8)]
            tokens = held[pl.ds(4 * g, 4 * count)].reshape(4 * CHUNK * count, depth)
            total[...] += jnp.dot(
                jnp.concatenate(pieces_of, axis=0).T, tokens, preferred_element_type=F32
            )

    def finish():
        for s in (steps - 2, steps - 1):
            wait_gradients(s)
        first = STEPS[steps - 2][0]
        count = len(GROUPS) - first
        g_t = gradients(first, count)
        span = depth // 4
        for i in range(4):
            ff = slice(i * span, (i + 1) * span)
            part = jnp.dot(g_t, tokens_of(first, count, ff), preferred_element_type=F32)
            grad[:, ff] = ((total[:, ff] + part) * keep[:, ff].astype(F32)).astype(BF16)
        arrived_bytes(placed, out_r)
        student_out[...] = placed[...].reshape(16 * PIECE, width).T

    stages = {"a": stage_a, "r": stage_r, "b": stage_b, "c": stage_c, "d": stage_d, "e": stage_e}

    for copy in t_cols:
        copy.start()
    start_tick(0)
    start_side(-1)
    t_own.start()
    for c in range(4):
        across[c].start()

    for tick in range(11):
        if tick:
            arrived = [ups[tick - 1], downs[tick - 1]]
            names = [SEND_UP[tick - 1][1], SEND_DOWN[tick - 1][1]]
            for i, at in enumerate(ARRIVE_SIDE):
                if at == tick:
                    arrived.append(sides[i])
                    names.append(SEND_SIDE[i][1])
            for copy, name in zip(arrived, names):
                copy.wait_recv()
                across[NUMBER[name]].start()
            start_tick(tick)
        for what in PLAN[tick]:
            if what == "x":
                start_side(tick)
            elif what == "w":
                sides[-1].wait_recv()
                across[-1].start()
            elif what == "rows":
                t_own.wait()
                arrived_bytes(cols.at[pl.ds(0, 15)], teacher_r.at[0])
                for copy in t_rows:
                    copy.start()
                targets[row] = cols[pl.ds(y * 4, 4)]
            elif what == "targets":
                arrived_bytes(targets.at[pl.ds(0, 7)], teacher_r.at[1])
            elif what == "q":
                quantize()
                for copy in own:
                    copy.wait()
            elif what == "f":
                finish()
            else:
                stages[what[0]](*map(int, what[1:]))

    for g in range(16):
        t, (here, there) = piece_copy(g)

        @pl.when(t != row)
        def _():
            there.wait_send()

    sums = LATE
    for i, ref in enumerate((
        held.at[pl.ds(0, len(SEND_UP) + len(SEND_DOWN) + len(SEND_SIDE) + len(ARRIVALS))],
        got_y.at[:, :, pl.ds(0, sums)],
        swap.at[pl.ds(0, sums)],
        got_y.at[:, :, pl.ds(0, sums)],
        swap.at[pl.ds(0, sums)],
        got_late,
        cols.at[pl.ds(0, 15)],
        targets.at[pl.ds(0, 7)],
        got_late,
    )):
        arrived_bytes(ref, sent.at[i])


def copy_out(student, grad, student_out, grad_out, sem):
    rows = grad.shape[0] // 6
    copies = [pltpu.make_async_copy(student, student_out, sem.at[6])]
    for i in range(6):
        part = pl.ds(i * rows, rows)
        copies.append(pltpu.make_async_copy(grad.at[part], grad_out.at[part], sem.at[i]))
    for copy in copies:
        copy.start()
    for copy in copies:
        copy.wait()


def local(hidden, weight, scale_exp, teacher):
    block, depth = hidden.shape
    width = weight.shape[1]
    tokens = block * lax.axis_size("col")
    groups, steps = len(GROUPS), len(STEPS)
    hidden = hidden.reshape(block // CHUNK, CHUNK, depth)
    dma = pltpu.SemaphoreType.DMA
    anywhere = pl.BlockSpec(memory_space=pl.ANY)
    student_out, grad = pl.pallas_call(
        functools.partial(kernel, 1.0 / math.sqrt(tokens)),
        out_shape=(
            pltpu.VMEM((width, 16 * PIECE), BF16),
            pltpu.VMEM((width, depth), BF16),
        ),
        in_specs=[anywhere, anywhere, pl.BlockSpec(memory_space=pltpu.SMEM), anywhere],
        out_specs=(pl.BlockSpec(memory_space=pltpu.VMEM),) * 2,
        scratch_shapes=[
            pltpu.VMEM((4 * groups, CHUNK, depth), BF16),
            pltpu.VMEM((width, depth), BF16),
            pltpu.VMEM((width, depth), BF16),
            pltpu.VMEM((width, depth), F32),
            pltpu.VMEM((16, depth), BF16),
            pltpu.VMEM((16, PIECE, width), BF16),
            pltpu.VMEM((4, 2, groups, PIECE, width), BF16),
            pltpu.VMEM((3, 2, groups, PIECE, width), BF16),
            pltpu.VMEM((groups, PIECE, width), BF16),
            pltpu.VMEM((groups, PIECE, width), BF16),
            pltpu.VMEM((7, groups - LATE, PIECE, width), BF16),
            pltpu.VMEM((4, 2, groups, PIECE, width), BF16),
            pltpu.VMEM((groups, PIECE, width), BF16),
            pltpu.VMEM((16, PIECE, width), BF16),
            pltpu.VMEM((16, PIECE, width), BF16),
            pltpu.VMEM((8, 4, PIECE, width), BF16),
            dma((6,)), dma((9,)), dma((10,)), dma((10,)), dma((8,)), dma((steps,)),
            dma((steps,)), dma((steps,)), dma((steps,)), dma((steps,)), dma((groups,)), dma, dma((2, steps - DIRECT)), dma((2,)),
        ],
        compiler_params=pltpu.CompilerParams(
            collective_id=0, has_side_effects=True, vmem_limit_bytes=60 * 2**20
        ),
        cost_estimate=pl.CostEstimate(
            flops=4 * tokens * depth * width, bytes_accessed=3 * depth * width, transcendentals=0
        ),
    )(hidden, weight.T, scale_exp.T, teacher)
    student_out, grad = pl.pallas_call(
        copy_out,
        out_shape=tuple(jax.ShapeDtypeStruct(a.shape, a.dtype) for a in (student_out, grad)),
        in_specs=[pl.BlockSpec(memory_space=pltpu.VMEM)] * 2,
        out_specs=(anywhere, anywhere),
        scratch_shapes=[dma((7,))],
        compiler_params=pltpu.CompilerParams(vmem_limit_bytes=8 * 2**20),
    )(student_out, grad)
    return (student_out.T, grad.T)


def solution(mesh):
    placed = (P("col", "row"), P("row", "col"), P("row", "col"), P(("row", "col"), None))
    return jax.shard_map(
        local,
        mesh=mesh,
        in_specs=placed,
        out_specs=(P("row", "col"), P("row", "col")),
        check_vma=False,
    )
```
